512 devices in a mesh: band: 16 (over x, z_hi, core), ga: 32 (over y, z_lo).
Axes of the slice: x: 4, y: 8, z: 8 (z_hi: 2, z_lo: 4; z = z_hi * 4 + z_lo), core: 2. Of those that a mesh axis runs over, the one named last changes fastest.
Arguments:
- psi_block: bfloat16 [16, 2048, 256], P('band', 'ga'), may hold values from -6 to 6
- potential: bfloat16 [256, 256, 256], P('ga'), may hold values from -2.5 to 1.5
- resident: bfloat16 [256, 2048, 256], P('band', 'ga'), may hold values from -0.013671875 to 0.013671875
- stick_cols: int32 [2048], P('ga'), may hold values from 0 to 65535, as said below
- stick_counts: int32 [2048], P('ga'), may hold values from 1 to 129, as said below
- plane_order: int32 [256], replicated, may hold values from 0 to 255, each once
Outputs:
- applied: bfloat16 [16, 2048, 256], P('band', 'ga')
- intersection: float32 [256, 16], P('band')
The draws below stay inside these ranges and needn't reach their ends.
Inputs may be any that keep to these rules, and one draw needn't show every extreme that they name: `stick_cols`: distinct columns kx * 256 + ky whose signed frequencies satisfy f(kx)^2 + f(ky)^2 <= 64^2; column 0, column (64) * 256 and column 65535 are always present. `stick_counts`: 2 h + 1, with h the largest integer such that h^2 + f(kx)^2 + f(ky)^2 <= 64^2 for the stick's column. `plane_order`: A permutation of the z-planes.
All inputs are finite; a program needn't handle non-finite values.
Results may differ from the reference program's by a relative error of at most 0.0072.
Values may be sent and summed in bfloat16 or wider, within the bound.
A program may use at most 64 MiB of HBM per device.

```python
import math
import jax
import jax.numpy as jnp
from jax import lax

GRID = 256
NB = 16
STICKS = 2048
RES = 256


def stick_layout(key):
    total_cells = GRID * GRID
    cell_index = jnp.arange(total_cells, dtype=jnp.int32)
    freq_x = cell_index // GRID
    freq_y = cell_index % GRID
    signed_x = jnp.where(freq_x < GRID // 2, freq_x, freq_x - GRID)
    signed_y = jnp.where(freq_y < GRID // 2, freq_y, freq_y - GRID)
    radius = GRID // 4
    remaining = radius * radius - signed_x * signed_x - signed_y * signed_y
    scores = jax.random.randint(key, (total_cells,), 0, 1024, dtype=jnp.int32) * total_cells + cell_index + 1
    forced = (cell_index == 0) | (cell_index == radius * GRID) | (cell_index == total_cells - 1)
    scores = jnp.where(forced, 1100 * total_cells + cell_index, scores)
    scores = jnp.where(remaining >= 0, scores, -1 - cell_index)
    picked = lax.top_k(scores, STICKS)[1].astype(jnp.int32)
    left_over = remaining[picked]
    steps_up = jnp.arange(1, radius + 1, dtype=jnp.int32)
    height = jnp.sum((steps_up[None, :] * steps_up[None, :] <= left_over[:, None]).astype(jnp.int32), axis=1)
    return (picked, 2 * height + 1)


def draw_stick_cols(key, part):
    layout = stick_layout(key)
    return layout[0]


def draw_stick_counts(key, part):
    layout = stick_layout(key)
    return layout[1]


def levels(key, extent, pieces, low, high):
    level = 1.0
    for axis_at, shards_of in pieces:
        heights = jax.random.uniform(jax.random.fold_in(jax.random.fold_in(key, 6), axis_at), (shards_of,), jnp.float32, low / len(pieces), high / len(pieces))
        level = level * jnp.repeat(jnp.exp(heights), extent[axis_at] // shards_of).reshape((-1,) + (1,) * (len(extent) - 1 - axis_at))
    return level


def normal_values(own_key, extent, scale, bound, shards=(), kind=jnp.bfloat16):
    drawn = scale * jax.random.normal(own_key, extent, jnp.float32)
    if shards:
        drawn = drawn * levels(own_key, extent, shards, -0.22, 0.18)
    return jnp.clip(drawn, -bound, bound).astype(kind)


def setup_inputs(seed: int = 0) -> dict:
    splits = jax.random.split(jax.random.key(seed), 7)
    psi_block = normal_values(splits[0], (NB, STICKS, GRID), 1.0, 6.0, ((0, 16), (1, 32)))
    potential = jnp.clip(-2.5 + 4.0 * jax.random.uniform(splits[1], (GRID, GRID, GRID), jnp.float32) ** levels(splits[1], (GRID, GRID, GRID), ((0, 32),), -0.2, 0.2), -2.5, 1.5).astype(jnp.bfloat16)
    resident = normal_values(splits[2], (RES, STICKS, GRID), (STICKS * GRID // 3) ** -0.5, 0.013671875, ((0, 16), (1, 32)))
    stick_cols = draw_stick_cols(jax.random.fold_in(splits[6], 71), 0)
    stick_counts = draw_stick_counts(jax.random.fold_in(splits[6], 71), 0)
    plane_order = jax.random.permutation(splits[5], GRID).astype(jnp.int32)
    return {"psi_block": psi_block, "potential": potential, "resident": resident, "stick_cols": stick_cols, "stick_counts": stick_counts, "plane_order": plane_order}


def hartley_table(row_index, col_index, grid_size):
    product = row_index[:, None] * col_index[None, :] % grid_size
    angle = product.astype(jnp.float32) * (2.0 * math.pi / grid_size)
    return ((jnp.cos(angle) + jnp.sin(angle)) * (1.0 / math.sqrt(grid_size))).astype(jnp.bfloat16)

def reference(psi_block, potential, resident, stick_cols, stick_counts, plane_order):
    frequency = jnp.arange(GRID, dtype=jnp.int32)
    grid_table = hartley_table(frequency, frequency, GRID)
    z_table = hartley_table(frequency, plane_order, GRID)
    signed_freq = jnp.where(frequency < GRID // 2, frequency, frequency - GRID)
    sphere = 2 * jnp.abs(signed_freq)[None, :] + 1 <= stick_counts[:, None]
    table_wide = grid_table.astype(jnp.float32)
    potential_wide = potential.astype(jnp.float32)

    def one_band(psi_rows):
        masked = jnp.where(sphere, psi_rows, jnp.zeros((), jnp.bfloat16))
        zreal = jnp.dot(z_table.T, masked.T, preferred_element_type=jnp.float32).astype(jnp.bfloat16)
        spread = jnp.zeros((GRID, GRID * GRID), jnp.bfloat16).at[:, stick_cols].set(zreal)
        spread = spread.reshape(GRID, GRID, GRID).astype(jnp.float32)
        halfway = jnp.einsum('kx,pkq->pxq', table_wide, spread).astype(jnp.bfloat16)
        field = jnp.einsum('pxq,qy->pxy', halfway.astype(jnp.float32), table_wide)
        weighted = (potential_wide * field).astype(jnp.bfloat16)
        backward = jnp.einsum('pxy,yq->pxq', weighted.astype(jnp.float32), table_wide).astype(jnp.bfloat16)
        spectrum = jnp.einsum('xk,pxq->pkq', table_wide, backward.astype(jnp.float32)).astype(jnp.bfloat16)
        picked = spectrum.reshape(GRID, GRID * GRID)[:, stick_cols]
        result = jnp.dot(picked.T, z_table.T, preferred_element_type=jnp.float32)
        return jnp.where(sphere, result, jnp.float32(0.0)).astype(jnp.bfloat16)
    applied = lax.map(one_band, psi_block)
    intersection = jnp.dot(resident.reshape(RES, STICKS * GRID), applied.reshape(NB, STICKS * GRID).T, preferred_element_type=jnp.float32)
    return (applied, intersection)
```

```python
import functools

import jax
import jax.numpy as jnp
import numpy as np
from jax import lax
from jax.experimental import pallas as pl
from jax.experimental.pallas import tpu as pltpu
from jax.sharding import PartitionSpec as P

MESH = pl.DeviceIdType.MESH
GRID = 256
RADIUS = 64
ROWS = 144
TILE = 256
F32 = jnp.float32
BF16 = jnp.bfloat16
EXACT = lax.Precision.HIGHEST


def hartley_tables():
    k = np.arange(GRID)
    angle = (k[:, None] * k[None, :] % GRID).astype(np.float32) * np.float32(2.0 * np.pi / GRID)
    table = ((np.cos(angle) + np.sin(angle)) * np.float32(1.0 / np.sqrt(GRID))).astype(BF16)
    disc = np.zeros((ROWS, GRID), BF16)
    disc[: 2 * RADIUS + 1] = table[np.arange(-RADIUS, RADIUS + 1) % GRID]
    return table, disc, np.ascontiguousarray(disc.T)


def iota(shape, axis):
    return lax.broadcasted_iota(jnp.int32, shape, axis)


def dot(a, b, ca, cb, precision=None):
    return lax.dot_general(
        a, b, (((ca,), (cb,)), ((), ())), precision=precision, preferred_element_type=F32
    )


def kernel(
    n_band,
    n_ga,
    psi_ref,
    pot_ref,
    res_ref,
    cols_ref,
    counts_ref,
    order_ref,
    table_ref,
    disc_ref,
    disc_t_ref,
    applied_ref,
    inter_ref,
    psi_v,
    pot_v,
    res_v,
    table_v,
    disc_v,
    disc_t_v,
    out_v,
    ztab_v,
    cols_send,
    cols_recv,
    z_send,
    z_recv,
    pick_send,
    pick_recv,
    onehot_x,
    table_y,
    half_acc,
    half_v,
    back_v,
    gather,
    red_send,
    red_recv,
    load_sem,
    send_sem,
    recv_sem,
    out_sem,
):
    me_b, me_g = lax.axis_index("band"), lax.axis_index("ga")
    sticks, planes = psi_ref.shape[0], pot_ref.shape[0]
    tiles = n_ga * sticks // TILE
    parity = lax.rem(me_g, 2)
    pairs = n_ga // 2

    loads = [
        pltpu.make_async_copy(src, dst, load_sem.at[i])
        for i, (src, dst) in enumerate(
            (
                (psi_ref, psi_v),
                (table_ref, table_v),
                (disc_ref, disc_v),
                (disc_t_ref, disc_t_v),
                (pot_ref, pot_v),
                (res_ref, res_v),
            )
        )
    ]
    for load in loads:
        load.start()

    barrier = pltpu.get_barrier_semaphore()

    @pl.loop(1, n_ga)
    def _(d):
        to = lax.rem(me_g + d, n_ga)
        pl.semaphore_signal(barrier, inc=1, device_id={"ga": to}, device_id_type=MESH)

    @pl.loop(1, n_band)
    def _(d):
        to = lax.rem(me_b + d, n_band)
        pl.semaphore_signal(barrier, inc=1, device_id={"band": to}, device_id_type=MESH)

    def send_ga(src, dst, phase, to):
        pltpu.make_async_remote_copy(
            src_ref=src,
            dst_ref=dst,
            send_sem=send_sem.at[phase],
            recv_sem=recv_sem.at[phase],
            device_id={"ga": to},
            device_id_type=MESH,
        ).start()

    def wait_bytes(ref, sem):
        pltpu.make_async_copy(ref, ref, sem).wait()

    counts = jnp.where(
        iota((sticks, sticks), 0) == iota((sticks, sticks), 1), counts_ref[...].astype(F32), 0.0
    ).sum(axis=1, keepdims=True)
    k = iota((sticks, GRID), 1)
    freq = jnp.where(k < GRID // 2, k, GRID - k)
    sphere = (2 * freq + 1).astype(F32) <= counts

    lane_half = iota((1, 2 * sticks), 1) // sticks
    own_half = lane_half == parity
    cols = cols_ref[...]
    cols_send[...] = jnp.where(own_half, jnp.concatenate([cols, cols], axis=1), 0)

    for load in loads[:4]:
        load.wait()
    order_pick = (iota((GRID, n_ga * planes), 0) == order_ref[...]).astype(F32).astype(BF16)
    ztab = dot(order_pick, table_v[...], 0, 0).astype(BF16)
    ztab_v[...] = ztab
    masked = jnp.where(sphere, psi_v[...].astype(F32), 0.0)
    two = jnp.concatenate(
        [jnp.where(parity == 0, masked, 0.0), jnp.where(parity == 1, masked, 0.0)], axis=0
    ).astype(BF16)
    zreal = dot(ztab, two, 1, 1).astype(BF16).astype(F32)
    z_send[...] = zreal.reshape(n_ga, planes, 2 * sticks)
    cols_recv[me_g] = cols_send[...]
    z_recv[me_g] = z_send[me_g]

    pl.semaphore_wait(barrier, n_ga + n_band - 2)

    @pl.loop(1, n_ga)
    def _(d):
        to = lax.rem(me_g + d, n_ga)
        send_ga(cols_send, cols_recv.at[me_g], 0, to)

    @pl.loop(1, n_ga)
    def _(d):
        to = lax.rem(me_g + d, n_ga)
        send_ga(z_send.at[to], z_recv.at[me_g], 1, to)

    wait_bytes(cols_recv.at[pl.ds(0, n_ga - 1)], recv_sem.at[0])

    @pl.loop(0, tiles)
    def _(t):
        col = jnp.concatenate(
            [cols_recv[4 * t] + cols_recv[4 * t + 1], cols_recv[4 * t + 2] + cols_recv[4 * t + 3]],
            axis=1,
        )
        kx, ky = lax.shift_right_logical(col, 8), col & (GRID - 1)
        row = jnp.where(kx < GRID // 2, kx + RADIUS, kx + RADIUS - GRID)
        onehot_x[t] = (iota((ROWS, TILE), 0) == row).astype(F32).astype(BF16)
        onehot_y = (iota((GRID, TILE), 0) == ky).astype(F32).astype(BF16)
        table_y[t] = dot(table_v[...], onehot_y, 1, 0).astype(BF16)

    wait_bytes(z_recv.at[pl.ds(0, n_ga - 1)], recv_sem.at[1])
    half_acc[...] = jnp.zeros_like(half_acc)

    @pl.loop(0, tiles)
    def _(t):
        z = jnp.concatenate(
            [z_recv[4 * t] + z_recv[4 * t + 1], z_recv[4 * t + 2] + z_recv[4 * t + 3]], axis=1
        )
        pick = onehot_x[t].reshape(ROWS // 16, 16, TILE)
        spread = jnp.concatenate(
            [
                (pick * jnp.broadcast_to(z[p : p + 1], (16, TILE)).astype(BF16)[None]).reshape(
                    ROWS, TILE
                )
                for p in range(planes)
            ],
            axis=0,
        )
        half_acc[...] += dot(spread, table_y[t], 1, 1)

    half_v[...] = half_acc[...].astype(BF16).reshape(planes, ROWS, GRID)
    loads[4].wait()

    @pl.loop(0, planes)
    def _(p):
        field = dot(disc_t_v[...], half_v[p], 1, 0)
        weighted = (pot_v[p].astype(F32) * field).astype(BF16)
        back_v[p] = dot(disc_v[...], weighted, 1, 0).astype(BF16)

    @pl.loop(0, tiles)
    def _(step):
        t = lax.rem(step + me_g // 4, tiles)
        spectrum = dot(back_v[...].reshape(planes * ROWS, GRID), table_y[t], 1, 0)
        picked = (spectrum.reshape(planes, ROWS, TILE) * onehot_x[t].astype(F32)[None]).sum(axis=1)
        picked = picked.astype(BF16).astype(F32)
        pick_send[2 * t] = picked[:, : 2 * sticks]
        pick_send[2 * t + 1] = picked[:, 2 * sticks :]
        for i in range(4):
            to = 4 * t + i

            @pl.when(to != me_g)
            def _():
                send_ga(pick_send.at[2 * t + i // 2], pick_recv.at[me_g], 2, to)

            @pl.when(to == me_g)
            def _():
                pick_recv[me_g] = pick_send[2 * t + i // 2]

    wait_bytes(pick_recv.at[pl.ds(0, n_ga - 1)], recv_sem.at[2])
    returned = jnp.where(own_half, pick_recv[...].reshape(n_ga * planes, 2 * sticks), 0.0)
    result = dot(returned.astype(BF16), ztab_v[...], 0, 0)
    result = result[:sticks] + result[sticks:]
    applied = jnp.where(sphere, result, 0.0).astype(BF16)
    out_v[...] = applied
    gather[me_b] = applied
    store = pltpu.make_async_copy(out_v, applied_ref, out_sem.at[0])
    store.start()

    @pl.loop(1, n_band)
    def _(d):
        to = lax.rem(me_b + d, n_band)
        pltpu.make_async_remote_copy(
            src_ref=out_v,
            dst_ref=gather.at[me_b],
            send_sem=send_sem.at[3],
            recv_sem=recv_sem.at[3],
            device_id={"band": to},
            device_id_type=MESH,
        ).start()

    loads[5].wait()
    wait_bytes(gather.at[pl.ds(0, n_band - 1)], recv_sem.at[3])
    n_res = res_v.shape[0]
    prod = jnp.zeros((n_res * 16, n_band * 16), F32)
    for g in range(sticks // 16):
        left = res_v[:, 16 * g : 16 * g + 16, :].reshape(n_res * 16, GRID)
        right = gather[:, 16 * g : 16 * g + 16, :].reshape(n_band * 16, GRID)
        prod += dot(left, right, 1, 1)
    same = iota(prod.shape, 0) % 16 == iota(prod.shape, 1) % 16
    summed = jnp.where(same, prod, 0.0).reshape(n_res, 16, n_band * 16).sum(axis=1)
    fold = (iota((n_band * 16, 128), 0) // 16 == iota((n_band * 16, 128), 1) % 16).astype(F32)
    part = dot(summed, fold, 1, 0, EXACT)
    part = jnp.where(iota(part.shape, 1) // 16 == iota(part.shape, 0) % 8, part, 0.0)
    red_send[...] = part.reshape(n_res // 8, 8, 128).sum(axis=1)
    red_recv[me_g] = red_send[...]

    @pl.loop(1, n_ga)
    def _(d):
        to = lax.rem(me_g + d, n_ga)
        send_ga(red_send, red_recv.at[me_g], 4, to)

    wait_bytes(red_recv.at[pl.ds(0, n_ga - 1)], recv_sem.at[4])
    inter_ref[...] = red_recv[...].sum(axis=0)

    store.wait()
    wait_bytes(cols_recv.at[pl.ds(0, n_ga - 1)], send_sem.at[0])
    wait_bytes(z_recv.at[pl.ds(0, n_ga - 1)], send_sem.at[1])
    wait_bytes(pick_recv.at[pl.ds(0, n_ga - 1)], send_sem.at[2])
    wait_bytes(gather.at[pl.ds(0, n_band - 1)], send_sem.at[3])
    wait_bytes(red_recv.at[pl.ds(0, n_ga - 1)], send_sem.at[4])


def body(n_band, n_ga, psi_block, potential, resident, stick_cols, stick_counts, plane_order):
    sticks, planes, n_res = psi_block.shape[1], potential.shape[0], resident.shape[0]
    tiles = n_ga * sticks // TILE
    table, disc, disc_t = hartley_tables()
    any_space = pl.BlockSpec(memory_space=pl.ANY)
    vmem = pl.BlockSpec(memory_space=pltpu.VMEM)
    applied, inter = pl.pallas_call(
        functools.partial(kernel, n_band, n_ga),
        out_shape=(
            jax.ShapeDtypeStruct((sticks, GRID), BF16),
            jax.ShapeDtypeStruct((n_res // 8, 128), F32),
        ),
        in_specs=[any_space] * 3 + [vmem] * 3 + [any_space] * 3,
        out_specs=(any_space, vmem),
        scratch_shapes=[
            pltpu.VMEM((sticks, GRID), BF16),
            pltpu.VMEM(potential.shape, BF16),
            pltpu.VMEM(resident.shape, BF16),
            pltpu.VMEM(table.shape, BF16),
            pltpu.VMEM(disc.shape, BF16),
            pltpu.VMEM(disc_t.shape, BF16),
            pltpu.VMEM((sticks, GRID), BF16),
            pltpu.VMEM((n_ga * planes, GRID), BF16),
            pltpu.VMEM((1, 2 * sticks), jnp.int32),
            pltpu.VMEM((n_ga, 1, 2 * sticks), jnp.int32),
            pltpu.VMEM((n_ga, planes, 2 * sticks), F32),
            pltpu.VMEM((n_ga, planes, 2 * sticks), F32),
            pltpu.VMEM((n_ga // 2, planes, 2 * sticks), F32),
            pltpu.VMEM((n_ga, planes, 2 * sticks), F32),
            pltpu.VMEM((tiles, ROWS, TILE), BF16),
            pltpu.VMEM((tiles, GRID, TILE), BF16),
            pltpu.VMEM((planes * ROWS, GRID), F32),
            pltpu.VMEM((planes, ROWS, GRID), BF16),
            pltpu.VMEM((planes, ROWS, GRID), BF16),
            pltpu.VMEM((n_band, sticks, GRID), BF16),
            pltpu.VMEM((n_res // 8, 128), F32),
            pltpu.VMEM((n_ga, n_res // 8, 128), F32),
            pltpu.SemaphoreType.DMA((6,)),
            pltpu.SemaphoreType.DMA((5,)),
            pltpu.SemaphoreType.DMA((5,)),
            pltpu.SemaphoreType.DMA((1,)),
        ],
        compiler_params=pltpu.CompilerParams(
            collective_id=0, has_side_effects=True, vmem_limit_bytes=40 * 2**20
        ),
    )(
        psi_block[0],
        potential,
        resident,
        stick_cols[None],
        stick_counts[None],
        plane_order[None],
        table,
        disc,
        disc_t,
    )
    return applied[None], inter.reshape(n_res, 16)[:, :n_band]


def solution(mesh):
    in_specs = (
        P("band", "ga", None),
        P("ga", None, None),
        P("band", "ga", None),
        P("ga"),
        P("ga"),
        P(),
    )
    out_specs = (P("band", "ga", None), P("band", None))
    step = functools.partial(body, mesh.shape["band"], mesh.shape["ga"])
    return jax.shard_map(step, mesh=mesh, in_specs=in_specs, out_specs=out_specs, check_vma=False)
```

```python
import functools

import jax
import jax.numpy as jnp
import numpy as np
from jax import lax
from jax.experimental import pallas as pl
from jax.experimental.pallas import tpu as pltpu
from jax.sharding import PartitionSpec as P

MESH = pl.DeviceIdType.MESH
GRID = 256
RADIUS = 64
ROWS = 144
TILE = 256
F32 = jnp.float32
BF16 = jnp.bfloat16
EXACT = lax.Precision.HIGHEST
UNROLL = 2
VMEM_BYTES = 60 * 2**20


def hartley_tables():
    k = np.arange(GRID)
    angle = (k[:, None] * k[None, :] % GRID).astype(np.float32) * np.float32(2.0 * np.pi / GRID)
    table = ((np.cos(angle) + np.sin(angle)) * np.float32(1.0 / np.sqrt(GRID))).astype(BF16)
    disc = np.zeros((ROWS, GRID), BF16)
    disc[: 2 * RADIUS + 1] = table[np.arange(-RADIUS, RADIUS + 1) % GRID]
    return table, disc, np.ascontiguousarray(disc.T)


def iota(shape, axis):
    return lax.broadcasted_iota(jnp.int32, shape, axis)


def dot(a, b, ca, cb, precision=None):
    return lax.dot_general(
        a, b, (((ca,), (cb,)), ((), ())), precision=precision, preferred_element_type=F32
    )


def kernel(
    n_band,
    n_ga,
    psi_ref,
    pot_ref,
    res_ref,
    cols_ref,
    counts_ref,
    order_ref,
    table_ref,
    disc_ref,
    disc_t_ref,
    applied_ref,
    inter_ref,
    cols_v,
    counts_v,
    order_v,
    psi_v,
    pot_v,
    res_v,
    table_v,
    disc_v,
    disc_t_v,
    out_v,
    ztab_v,
    cols_send,
    cols_recv,
    z_send,
    z_recv,
    pick_send,
    pick_recv,
    onehot_x,
    table_y,
    half_acc,
    half_v,
    back_v,
    packed_res,
    gather,
    red_send,
    red_recv,
    load_sem,
    send_sem,
    cols_sem,
    z_sem,
    pick_sem,
    gather_sem,
    red_sem,
    out_sem,
):
    me_b, me_g = lax.axis_index("band"), lax.axis_index("ga")
    sticks, planes, n_res = psi_ref.shape[0], pot_ref.shape[0], res_ref.shape[0]
    per_tile = TILE // sticks
    tiles = n_ga // per_tile
    me_t = me_g // per_tile
    core, column = me_b % 2, me_b // 2
    n_col = n_band // 2
    parity = lax.rem(me_g, 2)

    barrier = pltpu.get_barrier_semaphore()

    @pl.loop(1, n_ga)
    def _(d):
        to = lax.rem(me_g + d, n_ga)
        pl.semaphore_signal(barrier, inc=1, device_id={"ga": to}, device_id_type=MESH)

    @pl.loop(1, n_col)
    def _(d):
        to = lax.rem(column + d, n_col) * 2 + core
        pl.semaphore_signal(barrier, inc=1, device_id={"band": to}, device_id_type=MESH)

    other = column * 2 + 1 - core
    pl.semaphore_signal(barrier, inc=1, device_id={"band": other}, device_id_type=MESH)

    loads = [
        pltpu.make_async_copy(src, dst, load_sem.at[i])
        for i, (src, dst) in enumerate(
            (
                (cols_ref, cols_v),
                (counts_ref, counts_v),
                (order_ref, order_v),
                (psi_ref, psi_v),
                (table_ref, table_v),
                (disc_ref, disc_v),
                (disc_t_ref, disc_t_v),
                (pot_ref, pot_v),
                (res_ref, res_v),
            )
        )
    ]
    for load in loads:
        load.start()
    taken = set()

    def take(*which):
        for i in which:
            loads[i].wait()
            taken.add(i)

    def send(src, dst, phase, sem, **to):
        pltpu.make_async_remote_copy(
            src_ref=src,
            dst_ref=dst,
            send_sem=send_sem.at[phase],
            recv_sem=sem,
            device_id=to,
            device_id_type=MESH,
        ).start()

    def wait_bytes(ref, sem):
        pltpu.make_async_copy(ref, ref, sem).wait()

    def tile_at(step):
        ahead = jnp.where(step % 2 == 1, (step + 1) // 2, tiles - step // 2)
        return lax.rem(me_t + ahead, tiles)

    take(0, 1, 2)
    counts = jnp.where(
        iota((sticks, sticks), 0) == iota((sticks, sticks), 1), counts_v[...].astype(F32), 0.0
    ).sum(axis=1, keepdims=True)
    k = iota((sticks, GRID), 1)
    freq = jnp.where(k < GRID // 2, k, GRID - k)
    sphere = (2 * freq + 1).astype(F32) <= counts

    lane_half = iota((1, 2 * sticks), 1) // sticks
    own_half = lane_half == parity
    cols = cols_v[...]
    cols_send[...] = jnp.where(own_half, jnp.concatenate([cols, cols], axis=1), 0)
    pltpu.make_async_copy(cols_send, cols_recv.at[me_g], cols_sem.at[me_t]).start()

    take(3, 4)
    order_pick = (iota((GRID, n_ga * planes), 0) == order_v[...]).astype(F32).astype(BF16)
    ztab = dot(order_pick, table_v[...], 0, 0).astype(BF16)
    ztab_v[...] = ztab
    masked = jnp.where(sphere, psi_v[...].astype(F32), 0.0)
    two = jnp.concatenate(
        [jnp.where(parity == 0, masked, 0.0), jnp.where(parity == 1, masked, 0.0)], axis=0
    ).astype(BF16)
    zreal = dot(ztab, two, 1, 1).astype(BF16).astype(F32)
    z_send[...] = zreal.reshape(n_ga, planes, 2 * sticks)
    pltpu.make_async_copy(z_send.at[me_g], z_recv.at[me_g], z_sem.at[me_t]).start()
    half_acc[...] = jnp.zeros_like(half_acc)

    pl.semaphore_wait(barrier, n_ga - 1 + n_col)

    @pl.loop(1, n_ga)
    def _(d):
        to = lax.rem(me_g + n_ga // 2 + d, n_ga)
        to = jnp.where(to == me_g, lax.rem(me_g + n_ga // 2, n_ga), to)
        send(cols_send, cols_recv.at[me_g], 0, cols_sem.at[me_t], ga=to)
        send(z_send.at[to], z_recv.at[me_g], 1, z_sem.at[me_t], ga=to)

    @pl.loop(0, tiles)
    def _(step):
        t = tile_at(step)
        base = per_tile * t
        wait_bytes(cols_recv.at[pl.ds(base, per_tile)], cols_sem.at[t])
        col = jnp.concatenate(
            [cols_recv[base + i] + cols_recv[base + i + 1] for i in range(0, per_tile, 2)], axis=1
        )
        kx, ky = lax.shift_right_logical(col, 8), col & (GRID - 1)
        row = jnp.where(kx < GRID // 2, kx + RADIUS, kx + RADIUS - GRID)
        onehot_x[t] = (iota((ROWS, TILE), 0) == row).astype(F32).astype(BF16)
        onehot_y = (iota((GRID, TILE), 0) == ky).astype(F32).astype(BF16)
        table_y[t] = dot(table_v[...], onehot_y, 1, 0).astype(BF16)
        wait_bytes(z_recv.at[pl.ds(base, per_tile)], z_sem.at[t])
        z = jnp.concatenate(
            [z_recv[base + i] + z_recv[base + i + 1] for i in range(0, per_tile, 2)], axis=1
        )
        pick = onehot_x[t].reshape(ROWS // 16, 16, TILE)
        spread = jnp.concatenate(
            [
                (pick * jnp.broadcast_to(z[p : p + 1], (16, TILE)).astype(BF16)[None]).reshape(
                    ROWS, TILE
                )
                for p in range(planes)
            ],
            axis=0,
        )
        half_acc[...] += dot(spread, table_y[t], 1, 1)

    half_v[...] = half_acc[...].astype(BF16).reshape(planes, ROWS, GRID)
    take(5, 6, 7)

    @pl.loop(0, planes, unroll=UNROLL)
    def _(p):
        field = dot(disc_t_v[...], half_v[p], 1, 0)
        weighted = (pot_v[p].astype(F32) * field).astype(BF16)
        back_v[p] = dot(disc_v[...], weighted, 1, 0).astype(BF16)

    @pl.loop(0, tiles)
    def _(step):
        t = tile_at(tiles - 1 - step)
        spectrum = dot(back_v[...].reshape(planes * ROWS, GRID), table_y[t], 1, 0)
        picked = (spectrum.reshape(planes, ROWS, TILE) * onehot_x[t].astype(F32)[None]).sum(axis=1)
        picked = picked.astype(BF16).astype(F32)
        for i in range(per_tile // 2):
            pair = per_tile // 2 * t + i
            pick_send[pair] = picked[:, 2 * sticks * i : 2 * sticks * (i + 1)]
        for i in range(per_tile):
            to = per_tile * t + i

            @pl.when(to != me_g)
            def _():
                send(pick_send.at[to // 2], pick_recv.at[me_g], 2, pick_sem.at[0], ga=to)

    pltpu.make_async_copy(pick_send.at[me_g // 2], pick_recv.at[me_g], pick_sem.at[0]).start()

    def packed(low, high):
        lane = iota(low.shape, low.ndim - 1)
        spare = (lane == RADIUS) & (counts < 2 * RADIUS + 1)
        return jnp.where(
            lane < RADIUS, low, jnp.where(spare, pltpu.roll(low, 1, low.ndim - 2), high)
        )

    take(8)

    @pl.loop(0, n_res)
    def _(r):
        rows = res_v[r].astype(F32)
        packed_res[r] = packed(rows[:, : GRID // 2], rows[:, GRID // 2 :]).astype(BF16)

    wait_bytes(pick_recv, pick_sem.at[0])
    returned = jnp.where(own_half, pick_recv[...].reshape(n_ga * planes, 2 * sticks), 0.0)
    result = dot(returned.astype(BF16), ztab_v[...], 0, 0)
    result = jnp.where(sphere, result[:sticks] + result[sticks:], 0.0)
    gather[core, column] = packed(result[:, : GRID // 2], result[:, GRID // 2 :]).astype(BF16)

    for dz in range(min(2, n_col) - 1, -1, -1):
        for dx in [i for i in (2, 1, 3, 0) if i < n_col // 2 or i == 0]:
            if dx == 0 and dz == 0:
                continue
            q = column_of(column, n_col, dx, dz)
            slot = gather.at[core, column]
            send(slot, slot, 3, gather_sem.at[0, 2 * dx + dz], band=2 * q + core)
    slot = gather.at[core, column]
    send(slot, slot, 3, gather_sem.at[1, 0], band=other)
    out_v[...] = result.astype(BF16)
    store = pltpu.make_async_copy(out_v, applied_ref, out_sem.at[0])
    store.start()
    offsets = [
        (dx, dz)
        for dx, dz in ((1, 0), (3, 0), (0, 1), (2, 0), (1, 1), (3, 1), (2, 1))
        if (dx < n_col // 2 or dx == 0) and dz < n_col
    ]
    for dx, dz in offsets:
        q = column_of(column, n_col, -dx, dz)
        slot = gather.at[core, q]
        wait_bytes(slot, gather_sem.at[0, 2 * dx + dz])
        send(slot, slot, 3, gather_sem.at[1, 2 * dx + dz], band=other)

    def products(which):
        prod = jnp.zeros((n_res * 16, n_col * 16), F32)
        for g in range(sticks // 16):
            left = packed_res[:, 16 * g : 16 * g + 16, :].reshape(n_res * 16, GRID // 2)
            right = gather[which, :, 16 * g : 16 * g + 16, :].reshape(n_col * 16, GRID // 2)
            prod += dot(left, right, 1, 1)
        same = iota(prod.shape, 0) % 16 == iota(prod.shape, 1) % 16
        summed = jnp.where(same, prod, 0.0).reshape(n_res, 16, n_col * 16).sum(axis=1)
        band = iota((n_col * 16, 128), 0) // 16 * 2 + which
        fold = (band == iota((n_col * 16, 128), 1) % 16).astype(F32)
        return dot(summed, fold, 1, 0, EXACT)

    part = products(core)
    for dx, dz in [(0, 0)] + offsets:
        q = column_of(column, n_col, -dx, dz)
        wait_bytes(gather.at[1 - core, q], gather_sem.at[1, 2 * dx + dz])
    part += products(1 - core)
    part = jnp.where(iota(part.shape, 1) // 16 == iota(part.shape, 0) % 8, part, 0.0)
    red_send[...] = part.reshape(n_res // 8, 8, 128).sum(axis=1)
    pltpu.make_async_copy(red_send, red_recv.at[me_g], red_sem.at[0]).start()

    @pl.loop(1, n_ga)
    def _(d):
        to = lax.rem(me_g + d, n_ga)
        send(red_send, red_recv.at[me_g], 4, red_sem.at[0], ga=to)

    wait_bytes(red_recv, red_sem.at[0])
    inter_ref[...] = red_recv[...].sum(axis=0)

    store.wait()
    wait_bytes(cols_recv.at[pl.ds(0, n_ga - 1)], send_sem.at[0])
    wait_bytes(z_recv.at[pl.ds(0, n_ga - 1)], send_sem.at[1])
    wait_bytes(pick_recv.at[pl.ds(0, n_ga - 1)], send_sem.at[2])
    for _ in range(2):
        wait_bytes(gather.at[0, pl.ds(0, n_col - 1)], send_sem.at[3])
    wait_bytes(gather.at[0, 0], send_sem.at[3])
    wait_bytes(red_recv.at[pl.ds(0, n_ga - 1)], send_sem.at[4])


def column_of(column, n_col, dx, dz):
    if n_col == 1:
        return column
    n_x = n_col // 2
    x = lax.rem(column // 2 + dx + n_x, n_x)
    z = lax.rem(column % 2 + dz, 2)
    return 2 * x + z


def body(n_band, n_ga, psi_block, potential, resident, stick_cols, stick_counts, plane_order):
    sticks, planes, n_res = psi_block.shape[1], potential.shape[0], resident.shape[0]
    tiles = n_ga * sticks // TILE
    table, disc, disc_t = hartley_tables()
    hbm = pl.BlockSpec(memory_space=pltpu.HBM)
    vmem = pl.BlockSpec(memory_space=pltpu.VMEM)
    applied, inter = pl.pallas_call(
        functools.partial(kernel, n_band, n_ga),
        out_shape=(
            jax.ShapeDtypeStruct((sticks, GRID), BF16),
            jax.ShapeDtypeStruct((n_res // 8, 128), F32),
        ),
        in_specs=[hbm] * 9,
        out_specs=(hbm, vmem),
        scratch_shapes=[
            pltpu.VMEM((1, sticks), jnp.int32),
            pltpu.VMEM((1, sticks), jnp.int32),
            pltpu.VMEM((1, n_ga * planes), jnp.int32),
            pltpu.VMEM((sticks, GRID), BF16),
            pltpu.VMEM(potential.shape, BF16),
            pltpu.VMEM(resident.shape, BF16),
            pltpu.VMEM(table.shape, BF16),
            pltpu.VMEM(disc.shape, BF16),
            pltpu.VMEM(disc_t.shape, BF16),
            pltpu.VMEM((sticks, GRID), BF16),
            pltpu.VMEM((n_ga * planes, GRID), BF16),
            pltpu.VMEM((1, 2 * sticks), jnp.int32),
            pltpu.VMEM((n_ga, 1, 2 * sticks), jnp.int32),
            pltpu.VMEM((n_ga, planes, 2 * sticks), F32),
            pltpu.VMEM((n_ga, planes, 2 * sticks), F32),
            pltpu.VMEM((n_ga // 2, planes, 2 * sticks), F32),
            pltpu.VMEM((n_ga, planes, 2 * sticks), F32),
            pltpu.VMEM((tiles, ROWS, TILE), BF16),
            pltpu.VMEM((tiles, GRID, TILE), BF16),
            pltpu.VMEM((planes * ROWS, GRID), F32),
            pltpu.VMEM((planes, ROWS, GRID), BF16),
            pltpu.VMEM((planes, ROWS, GRID), BF16),
            pltpu.VMEM((n_res, sticks, GRID // 2), BF16),
            pltpu.VMEM((2, n_band // 2, sticks, GRID // 2), BF16),
            pltpu.VMEM((n_res // 8, 128), F32),
            pltpu.VMEM((n_ga, n_res // 8, 128), F32),
            pltpu.SemaphoreType.DMA((9,)),
            pltpu.SemaphoreType.DMA((5,)),
            pltpu.SemaphoreType.DMA((tiles,)),
            pltpu.SemaphoreType.DMA((tiles,)),
            pltpu.SemaphoreType.DMA((1,)),
            pltpu.SemaphoreType.DMA((2, 8)),
            pltpu.SemaphoreType.DMA((1,)),
            pltpu.SemaphoreType.DMA((1,)),
        ],
        compiler_params=pltpu.CompilerParams(
            collective_id=0, has_side_effects=True, vmem_limit_bytes=VMEM_BYTES
        ),
    )(
        psi_block[0],
        potential,
        resident,
        stick_cols[None],
        stick_counts[None],
        plane_order[None],
        table,
        disc,
        disc_t,
    )
    return applied[None], inter.reshape(n_res, 16)[:, :n_band]


def solution(mesh):
    in_specs = (
        P("band", "ga", None),
        P("ga", None, None),
        P("band", "ga", None),
        P("ga"),
        P("ga"),
        P(),
    )
    out_specs = (P("band", "ga", None), P("band", None))
    step = functools.partial(body, mesh.shape["band"], mesh.shape["ga"])
    return jax.shard_map(step, mesh=mesh, in_specs=in_specs, out_specs=out_specs, check_vma=False)
```

```python
import functools

import jax
import jax.numpy as jnp
import numpy as np
from jax import lax
from jax.experimental import pallas as pl
from jax.experimental.pallas import tpu as pltpu
from jax.sharding import PartitionSpec as P

MESH = pl.DeviceIdType.MESH
GRID = 256
RADIUS = 64
ROWS = 144
TILE = 256
F32 = jnp.float32
BF16 = jnp.bfloat16
EXACT = lax.Precision.HIGHEST
UNROLL = 4
VMEM_BYTES = 60 * 2**20


def hartley_tables():
    k = np.arange(GRID)
    angle = (k[:, None] * k[None, :] % GRID).astype(np.float32) * np.float32(2.0 * np.pi / GRID)
    table = ((np.cos(angle) + np.sin(angle)) * np.float32(1.0 / np.sqrt(GRID))).astype(BF16)
    disc = np.zeros((ROWS, GRID), BF16)
    disc[: 2 * RADIUS + 1] = table[np.arange(-RADIUS, RADIUS + 1) % GRID]
    return table, disc, np.ascontiguousarray(disc.T)


def iota(shape, axis):
    return lax.broadcasted_iota(jnp.int32, shape, axis)


def dot(a, b, ca, cb, precision=None):
    return lax.dot_general(
        a, b, (((ca,), (cb,)), ((), ())), precision=precision, preferred_element_type=F32
    )


def kernel(
    n_band,
    n_ga,
    psi_ref,
    pot_ref,
    res_ref,
    cols_ref,
    counts_ref,
    order_ref,
    table_ref,
    disc_ref,
    disc_t_ref,
    applied_ref,
    red_recv,
    cols_v,
    counts_v,
    order_v,
    psi_v,
    pot_v,
    res_v,
    table_v,
    disc_v,
    disc_t_v,
    out_v,
    ztab_v,
    cols_send,
    cols_recv,
    z_send,
    z_recv,
    pick_send,
    pick_recv,
    onehot_x,
    table_y,
    half_acc,
    half_v,
    back_v,
    packed_res,
    gather,
    red_send,
    load_sem,
    send_sem,
    cols_sem,
    z_sem,
    pick_sem,
    gather_sem,
    red_sem,
    out_sem,
):
    me_b, me_g = lax.axis_index("band"), lax.axis_index("ga")
    sticks, planes, n_res = psi_ref.shape[0], pot_ref.shape[0], res_ref.shape[0]
    per_tile = TILE // sticks
    tiles = n_ga // per_tile
    me_t = me_g // per_tile
    core, column = me_b % 2, me_b // 2
    n_col = n_band // 2
    parity = lax.rem(me_g, 2)

    barrier = pltpu.get_barrier_semaphore()

    @pl.loop(1, n_ga)
    def _(d):
        to = lax.rem(me_g + d, n_ga)
        pl.semaphore_signal(barrier, inc=1, device_id={"ga": to}, device_id_type=MESH)

    @pl.loop(1, n_col)
    def _(d):
        to = lax.rem(column + d, n_col) * 2 + core
        pl.semaphore_signal(barrier, inc=1, device_id={"band": to}, device_id_type=MESH)

    other = column * 2 + 1 - core
    pl.semaphore_signal(barrier, inc=1, device_id={"band": other}, device_id_type=MESH)

    loads = [
        pltpu.make_async_copy(src, dst, load_sem.at[i])
        for i, (src, dst) in enumerate(
            (
                (cols_ref, cols_v),
                (counts_ref, counts_v),
                (order_ref, order_v),
                (psi_ref, psi_v),
                (table_ref, table_v),
                (disc_ref, disc_v),
                (disc_t_ref, disc_t_v),
                (pot_ref, pot_v),
                (res_ref, res_v),
            )
        )
    ]
    for load in loads:
        load.start()
    taken = set()

    def take(*which):
        for i in which:
            loads[i].wait()
            taken.add(i)

    def send(src, dst, phase, sem, **to):
        pltpu.make_async_remote_copy(
            src_ref=src,
            dst_ref=dst,
            send_sem=send_sem.at[phase],
            recv_sem=sem,
            device_id=to,
            device_id_type=MESH,
        ).start()

    def wait_bytes(ref, sem):
        pltpu.make_async_copy(ref, ref, sem).wait()

    def swap(even, odd):
        low = iota(even.shape, 1) < sticks
        lower = jnp.where(low, even, pltpu.roll(odd, sticks, 1))
        upper = jnp.where(low, pltpu.roll(even, sticks, 1), odd)
        return jnp.concatenate([lower, upper], axis=0)

    def z_pair(i):
        return z_recv[i], z_recv[i + 1]

    def tile_at(step):
        ahead = jnp.where(step % 2 == 1, (step + 1) // 2, tiles - step // 2)
        return lax.rem(me_t + ahead, tiles)

    take(0, 1, 2)
    counts = jnp.where(
        iota((sticks, sticks), 0) == iota((sticks, sticks), 1), counts_v[...].astype(F32), 0.0
    ).sum(axis=1, keepdims=True)
    k = iota((sticks, GRID), 1)
    freq = jnp.where(k < GRID // 2, k, GRID - k)
    sphere = (2 * freq + 1).astype(F32) <= counts

    lane_half = iota((1, 2 * sticks), 1) // sticks
    own_half = lane_half == parity
    cols = cols_v[...]
    cols_send[...] = jnp.where(own_half, jnp.concatenate([cols, cols], axis=1), 0)
    pltpu.make_async_copy(cols_send, cols_recv.at[me_g], cols_sem.at[me_t]).start()

    take(3, 4)
    n_planes, half = n_ga * planes, planes // 2
    q = iota((n_planes, n_planes), 1)
    moved = q % (n_planes // 2) // half * planes + q // (n_planes // 2) * half + q % half
    move = (iota((n_planes, n_planes), 0) == moved).astype(F32).astype(BF16)
    order = jnp.broadcast_to(order_v[...].astype(F32).astype(BF16), (16, n_planes))
    order = dot(order, move, 1, 0)[:1].astype(jnp.int32)
    order_pick = (iota((GRID, n_planes), 0) == order).astype(F32).astype(BF16)
    ztab = dot(order_pick, table_v[...], 0, 0).astype(BF16)
    ztab_v[...] = ztab
    masked = jnp.where(sphere, psi_v[...].astype(F32), 0.0).astype(BF16)
    zreal = dot(ztab, masked, 1, 1).astype(BF16).astype(F32)
    zreal = jnp.concatenate([zreal[: n_planes // 2], zreal[n_planes // 2 :]], axis=1)
    z_send[...] = zreal.reshape(n_ga, half, 2 * sticks)
    pltpu.make_async_copy(z_send.at[me_g], z_recv.at[me_g], z_sem.at[me_t]).start()
    half_acc[...] = jnp.zeros_like(half_acc)

    pl.semaphore_wait(barrier, n_ga - 1 + n_col)

    @pl.loop(1, n_ga)
    def _(d):
        to = lax.rem(me_g + n_ga // 2 + d, n_ga)
        to = jnp.where(to == me_g, lax.rem(me_g + n_ga // 2, n_ga), to)
        send(cols_send, cols_recv.at[me_g], 0, cols_sem.at[me_t], ga=to)
        send(z_send.at[to], z_recv.at[me_g], 1, z_sem.at[me_t], ga=to)

    @pl.loop(0, tiles)
    def _(step):
        t = tile_at(step)
        base = per_tile * t
        wait_bytes(cols_recv.at[pl.ds(base, per_tile)], cols_sem.at[t])
        col = jnp.concatenate(
            [cols_recv[base + i] + cols_recv[base + i + 1] for i in range(0, per_tile, 2)], axis=1
        )
        kx, ky = lax.shift_right_logical(col, 8), col & (GRID - 1)
        row = jnp.where(kx < GRID // 2, kx + RADIUS, kx + RADIUS - GRID)
        onehot_x[t] = (iota((ROWS, TILE), 0) == row).astype(F32).astype(BF16)
        onehot_y = (iota((GRID, TILE), 0) == ky).astype(F32).astype(BF16)
        table_y[t] = dot(table_v[...], onehot_y, 1, 0).astype(BF16)
        wait_bytes(z_recv.at[pl.ds(base, per_tile)], z_sem.at[t])
        z = jnp.concatenate([swap(*z_pair(base + i)) for i in range(0, per_tile, 2)], axis=1)
        pick = onehot_x[t].reshape(ROWS // 16, 16, TILE)
        spread = jnp.concatenate(
            [
                (pick * jnp.broadcast_to(z[p : p + 1], (16, TILE)).astype(BF16)[None]).reshape(
                    ROWS, TILE
                )
                for p in range(planes)
            ],
            axis=0,
        )
        half_acc[...] += dot(spread, table_y[t], 1, 1)

    half_v[...] = half_acc[...].astype(BF16).reshape(planes, ROWS, GRID)
    take(5, 6, 7)

    @pl.loop(0, planes, unroll=UNROLL)
    def _(p):
        field = dot(disc_t_v[...], half_v[p], 1, 0)
        weighted = (pot_v[p].astype(F32) * field).astype(BF16)
        back_v[p] = dot(disc_v[...], weighted, 1, 0).astype(BF16)

    @pl.loop(0, tiles)
    def _(step):
        t = tile_at(tiles - 1 - step)
        spectrum = dot(back_v[...].reshape(planes * ROWS, GRID), table_y[t], 1, 0)
        picked = (spectrum.reshape(planes, ROWS, TILE) * onehot_x[t].astype(F32)[None]).sum(axis=1)
        picked = picked.astype(BF16).astype(F32)
        for i in range(per_tile // 2):
            pair = per_tile // 2 * t + i
            rows = picked[:, 2 * sticks * i : 2 * sticks * (i + 1)]
            low = iota((half, 2 * sticks), 1) < sticks
            lower, upper = rows[:half], rows[half:]
            pick_send[2 * pair] = jnp.where(low, lower, pltpu.roll(upper, sticks, 1))
            pick_send[2 * pair + 1] = jnp.where(low, pltpu.roll(lower, sticks, 1), upper)
        for i in range(per_tile):
            to = per_tile * t + i

            @pl.when(to != me_g)
            def _():
                send(pick_send.at[to], pick_recv.at[me_g], 2, pick_sem.at[0], ga=to)

    pltpu.make_async_copy(pick_send.at[me_g], pick_recv.at[me_g], pick_sem.at[0]).start()

    def packed(low, high):
        lane = iota(low.shape, low.ndim - 1)
        spare = (lane == RADIUS) & (counts < 2 * RADIUS + 1)
        return jnp.where(
            lane < RADIUS, low, jnp.where(spare, pltpu.roll(low, 1, low.ndim - 2), high)
        )

    take(8)

    @pl.loop(0, n_res)
    def _(r):
        rows = res_v[r].astype(F32)
        packed_res[r] = packed(rows[:, : GRID // 2], rows[:, GRID // 2 :]).astype(BF16)

    wait_bytes(pick_recv, pick_sem.at[0])
    returned = pick_recv[...].reshape(n_planes // 2, 2 * sticks)
    returned = jnp.concatenate([returned[:, :sticks], returned[:, sticks:]], axis=0)
    result = dot(returned.astype(BF16), ztab_v[...], 0, 0)
    result = jnp.where(sphere, result, 0.0)
    gather[core, column] = packed(result[:, : GRID // 2], result[:, GRID // 2 :]).astype(BF16)

    for dz in range(min(2, n_col) - 1, -1, -1):
        for dx in [i for i in (2, 1, 3, 0) if i < n_col // 2 or i == 0]:
            if dx == 0 and dz == 0:
                continue
            q = column_of(column, n_col, dx, dz)
            slot = gather.at[core, column]
            send(slot, slot, 3, gather_sem.at[0, 2 * dx + dz], band=2 * q + core)
    slot = gather.at[core, column]
    send(slot, slot, 3, gather_sem.at[1, 0], band=other)
    out_v[...] = result.astype(BF16)
    store = pltpu.make_async_copy(out_v, applied_ref, out_sem.at[0])
    store.start()
    offsets = [
        (dx, dz)
        for dx, dz in ((1, 0), (3, 0), (0, 1), (2, 0), (1, 1), (3, 1), (2, 1))
        if (dx < n_col // 2 or dx == 0) and dz < n_col
    ]
    for dx, dz in offsets:
        q = column_of(column, n_col, -dx, dz)
        slot = gather.at[core, q]
        wait_bytes(slot, gather_sem.at[0, 2 * dx + dz])
        send(slot, slot, 3, gather_sem.at[1, 2 * dx + dz], band=other)

    def products(which):
        prod = jnp.zeros((n_res * 16, n_col * 16), F32)
        for g in range(sticks // 16):
            left = packed_res[:, 16 * g : 16 * g + 16, :].reshape(n_res * 16, GRID // 2)
            right = gather[which, :, 16 * g : 16 * g + 16, :].reshape(n_col * 16, GRID // 2)
            prod += dot(left, right, 1, 1)
        same = iota(prod.shape, 0) % 16 == iota(prod.shape, 1) % 16
        summed = jnp.where(same, prod, 0.0).reshape(n_res, 16, n_col * 16).sum(axis=1)
        band = iota((n_col * 16, 128), 0) // 16 * 2 + which
        fold = (band == iota((n_col * 16, 128), 1) % 16).astype(F32)
        return dot(summed, fold, 1, 0, EXACT)

    part = products(core)
    for dx, dz in [(0, 0)] + offsets:
        q = column_of(column, n_col, -dx, dz)
        wait_bytes(gather.at[1 - core, q], gather_sem.at[1, 2 * dx + dz])
    part += products(1 - core)
    part = jnp.where(iota(part.shape, 1) // 16 == iota(part.shape, 0) % 8, part, 0.0)
    red_send[...] = part.reshape(n_res // 8, 8, 128).sum(axis=1)
    pltpu.make_async_copy(red_send, red_recv.at[me_g], red_sem.at[0]).start()

    @pl.loop(1, n_ga)
    def _(d):
        to = lax.rem(me_g + d, n_ga)
        send(red_send, red_recv.at[me_g], 4, red_sem.at[0], ga=to)

    wait_bytes(red_recv, red_sem.at[0])
    store.wait()
    wait_bytes(cols_recv.at[pl.ds(0, n_ga - 1)], send_sem.at[0])
    wait_bytes(z_recv.at[pl.ds(0, n_ga - 1)], send_sem.at[1])
    wait_bytes(pick_recv.at[pl.ds(0, n_ga - 1)], send_sem.at[2])
    for _ in range(2):
        wait_bytes(gather.at[0, pl.ds(0, n_col - 1)], send_sem.at[3])
    wait_bytes(gather.at[0, 0], send_sem.at[3])
    wait_bytes(red_recv.at[pl.ds(0, n_ga - 1)], send_sem.at[4])


def column_of(column, n_col, dx, dz):
    if n_col == 1:
        return column
    n_x = n_col // 2
    x = lax.rem(column // 2 + dx + n_x, n_x)
    z = lax.rem(column % 2 + dz, 2)
    return 2 * x + z


def finish(applied_ref, parts_ref, applied_out, inter_out):
    applied_out[0] = applied_ref[...]
    n_res = inter_out.shape[0]
    total = parts_ref[...].sum(axis=0)
    total = jnp.broadcast_to(total[:, None, :], (n_res // 8, 8, 128)).reshape(n_res, 128)
    total = jnp.where(iota(total.shape, 1) // 16 == iota(total.shape, 0) % 8, total, 0.0)
    fold = (iota((128, 16), 0) % 16 == iota((128, 16), 1)).astype(F32)
    inter_out[...] = dot(total, fold, 1, 0, EXACT)


def body(n_band, n_ga, psi_block, potential, resident, stick_cols, stick_counts, plane_order):
    sticks, planes, n_res = psi_block.shape[1], potential.shape[0], resident.shape[0]
    tiles = n_ga * sticks // TILE
    table, disc, disc_t = hartley_tables()
    hbm = pl.BlockSpec(memory_space=pltpu.HBM)
    vmem = pl.BlockSpec(memory_space=pltpu.VMEM)
    applied, inter = pl.pallas_call(
        functools.partial(kernel, n_band, n_ga),
        out_shape=(
            jax.ShapeDtypeStruct((sticks, GRID), BF16),
            jax.ShapeDtypeStruct((n_ga, n_res // 8, 128), F32),
        ),
        in_specs=[hbm] * 9,
        out_specs=(hbm, hbm),
        scratch_shapes=[
            pltpu.VMEM((1, sticks), jnp.int32),
            pltpu.VMEM((1, sticks), jnp.int32),
            pltpu.VMEM((1, n_ga * planes), jnp.int32),
            pltpu.VMEM((sticks, GRID), BF16),
            pltpu.VMEM(potential.shape, BF16),
            pltpu.VMEM(resident.shape, BF16),
            pltpu.VMEM(table.shape, BF16),
            pltpu.VMEM(disc.shape, BF16),
            pltpu.VMEM(disc_t.shape, BF16),
            pltpu.VMEM((sticks, GRID), BF16),
            pltpu.VMEM((n_ga * planes, GRID), BF16),
            pltpu.VMEM((1, 2 * sticks), jnp.int32),
            pltpu.VMEM((n_ga, 1, 2 * sticks), jnp.int32),
            pltpu.VMEM((n_ga, planes // 2, 2 * sticks), F32),
            pltpu.VMEM((n_ga, planes // 2, 2 * sticks), F32),
            pltpu.VMEM((n_ga, planes // 2, 2 * sticks), F32),
            pltpu.VMEM((n_ga, planes // 2, 2 * sticks), F32),
            pltpu.VMEM((tiles, ROWS, TILE), BF16),
            pltpu.VMEM((tiles, GRID, TILE), BF16),
            pltpu.VMEM((planes * ROWS, GRID), F32),
            pltpu.VMEM((planes, ROWS, GRID), BF16),
            pltpu.VMEM((planes, ROWS, GRID), BF16),
            pltpu.VMEM((n_res, sticks, GRID // 2), BF16),
            pltpu.VMEM((2, n_band // 2, sticks, GRID // 2), BF16),
            pltpu.VMEM((n_res // 8, 128), F32),
            pltpu.SemaphoreType.DMA((9,)),
            pltpu.SemaphoreType.DMA((5,)),
            pltpu.SemaphoreType.DMA((tiles,)),
            pltpu.SemaphoreType.DMA((tiles,)),
            pltpu.SemaphoreType.DMA((1,)),
            pltpu.SemaphoreType.DMA((2, 8)),
            pltpu.SemaphoreType.DMA((1,)),
            pltpu.SemaphoreType.DMA((1,)),
        ],
        compiler_params=pltpu.CompilerParams(
            collective_id=0, has_side_effects=True, vmem_limit_bytes=VMEM_BYTES
        ),
    )(
        psi_block[0],
        potential,
        resident,
        stick_cols[None],
        stick_counts[None],
        plane_order[None],
        table,
        disc,
        disc_t,
    )
    applied, inter = pl.pallas_call(
        finish,
        out_shape=(
            jax.ShapeDtypeStruct((1, sticks, GRID), BF16),
            jax.ShapeDtypeStruct((n_res, 16), F32),
        ),
        in_specs=[vmem] * 2,
        out_specs=(vmem, vmem),
    )(applied, inter)
    return applied, inter[:, :n_band]


def solution(mesh):
    in_specs = (
        P("band", "ga", None),
        P("ga", None, None),
        P("band", "ga", None),
        P("ga"),
        P("ga"),
        P(),
    )
    out_specs = (P("band", "ga", None), P("band", None))
    step = functools.partial(body, mesh.shape["band"], mesh.shape["ga"])
    return jax.shard_map(step, mesh=mesh, in_specs=in_specs, out_specs=out_specs, check_vma=False)
```

```python
import functools

import jax
import jax.numpy as jnp
import numpy as np
from jax import lax
from jax.experimental import pallas as pl
from jax.experimental.pallas import tpu as pltpu
from jax.sharding import PartitionSpec as P

MESH = pl.DeviceIdType.MESH
GRID = 256
RADIUS = 64
ROWS = 144
TILE = 256
F32 = jnp.float32
BF16 = jnp.bfloat16
EXACT = lax.Precision.HIGHEST
UNROLL = 4
VMEM_BYTES = 60 * 2**20


def hartley_tables():
    k = np.arange(GRID)
    angle = (k[:, None] * k[None, :] % GRID).astype(np.float32) * np.float32(2.0 * np.pi / GRID)
    table = ((np.cos(angle) + np.sin(angle)) * np.float32(1.0 / np.sqrt(GRID))).astype(BF16)
    disc = np.zeros((ROWS, GRID), BF16)
    disc[: 2 * RADIUS + 1] = table[np.arange(-RADIUS, RADIUS + 1) % GRID]
    return table, disc, np.ascontiguousarray(disc.T)


def iota(shape, axis):
    return lax.broadcasted_iota(jnp.int32, shape, axis)


def dot(a, b, ca, cb, precision=None):
    return lax.dot_general(
        a, b, (((ca,), (cb,)), ((), ())), precision=precision, preferred_element_type=F32
    )


def kernel(
    n_band,
    n_ga,
    psi_ref,
    pot_ref,
    res_ref,
    cols_ref,
    counts_ref,
    order_ref,
    table_ref,
    disc_ref,
    disc_t_ref,
    applied_ref,
    red_recv,
    cols_v,
    counts_v,
    order_v,
    psi_v,
    pot_v,
    res_v,
    table_v,
    disc_v,
    disc_t_v,
    out_v,
    ztab_v,
    cols_send,
    cols_recv,
    z_send,
    z_recv,
    pick_send,
    pick_recv,
    onehot_x,
    table_y,
    half_acc,
    back_v,
    packed_res,
    gather,
    red_send,
    load_sem,
    send_sem,
    cols_sem,
    z_sem,
    pick_sem,
    gather_sem,
    red_sem,
    out_sem,
):
    me_b, me_g = lax.axis_index("band"), lax.axis_index("ga")
    sticks, planes, n_res = psi_ref.shape[0], pot_ref.shape[0], res_ref.shape[0]
    per_tile = TILE // sticks
    tiles = n_ga // per_tile
    me_t = me_g // per_tile
    core, column = me_b % 2, me_b // 2
    n_col = n_band // 2
    parity = lax.rem(me_g, 2)

    barrier = pltpu.get_barrier_semaphore()

    @pl.loop(1, n_ga)
    def _(d):
        to = lax.rem(me_g + d, n_ga)
        pl.semaphore_signal(barrier, inc=1, device_id={"ga": to}, device_id_type=MESH)

    @pl.loop(1, n_col)
    def _(d):
        to = lax.rem(column + d, n_col) * 2 + core
        pl.semaphore_signal(barrier, inc=1, device_id={"band": to}, device_id_type=MESH)

    other = column * 2 + 1 - core
    pl.semaphore_signal(barrier, inc=1, device_id={"band": other}, device_id_type=MESH)

    loads = [
        pltpu.make_async_copy(src, dst, load_sem.at[i])
        for i, (src, dst) in enumerate(
            (
                (cols_ref, cols_v),
                (counts_ref, counts_v),
                (order_ref, order_v),
                (psi_ref, psi_v),
                (table_ref, table_v),
                (disc_ref, disc_v),
                (disc_t_ref, disc_t_v),
                (pot_ref, pot_v),
                (res_ref, res_v),
            )
        )
    ]
    for load in loads:
        load.start()
    taken = set()

    def take(*which):
        for i in which:
            loads[i].wait()
            taken.add(i)

    def send(src, dst, phase, sem, **to):
        pltpu.make_async_remote_copy(
            src_ref=src,
            dst_ref=dst,
            send_sem=send_sem.at[phase],
            recv_sem=sem,
            device_id=to,
            device_id_type=MESH,
        ).start()

    def wait_bytes(ref, sem):
        pltpu.make_async_copy(ref, ref, sem).wait()

    def swap(even, odd):
        low = iota(even.shape, 1) < sticks
        lower = jnp.where(low, even, pltpu.roll(odd, sticks, 1))
        upper = jnp.where(low, pltpu.roll(even, sticks, 1), odd)
        return jnp.concatenate([lower, upper], axis=0)

    def z_pair(i):
        return z_recv[i], z_recv[i + 1]

    def tile_at(step):
        ahead = jnp.where(step % 2 == 1, (step + 1) // 2, tiles - step // 2)
        return lax.rem(me_t + ahead, tiles)

    take(0, 1, 2)
    counts = jnp.where(
        iota((sticks, sticks), 0) == iota((sticks, sticks), 1), counts_v[...].astype(F32), 0.0
    ).sum(axis=1, keepdims=True)
    k = iota((sticks, GRID), 1)
    freq = jnp.where(k < GRID // 2, k, GRID - k)
    sphere = (2 * freq + 1).astype(F32) <= counts

    lane_half = iota((1, 2 * sticks), 1) // sticks
    own_half = lane_half == parity
    cols = cols_v[...]
    cols_send[...] = jnp.where(own_half, jnp.concatenate([cols, cols], axis=1), 0)
    pltpu.make_async_copy(cols_send, cols_recv.at[me_g], cols_sem.at[me_t]).start()

    take(3, 4)
    n_planes, half = n_ga * planes, planes // 2
    q = iota((n_planes, n_planes), 1)
    moved = q % (n_planes // 2) // half * planes + q // (n_planes // 2) * half + q % half
    move = (iota((n_planes, n_planes), 0) == moved).astype(F32).astype(BF16)
    order = jnp.broadcast_to(order_v[...].astype(F32).astype(BF16), (16, n_planes))
    order = dot(order, move, 1, 0)[:1].astype(jnp.int32)
    order_pick = (iota((GRID, n_planes), 0) == order).astype(F32).astype(BF16)
    ztab = dot(order_pick, table_v[...], 0, 0).astype(BF16)
    ztab_v[...] = ztab
    masked = jnp.where(sphere, psi_v[...].astype(F32), 0.0).astype(BF16)
    zreal = dot(ztab, masked, 1, 1).astype(BF16).astype(F32)
    zreal = jnp.concatenate([zreal[: n_planes // 2], zreal[n_planes // 2 :]], axis=1)
    z_send[...] = zreal.reshape(n_ga, half, 2 * sticks)
    pltpu.make_async_copy(z_send.at[me_g], z_recv.at[me_g], z_sem.at[me_t]).start()
    half_acc[...] = jnp.zeros_like(half_acc)

    pl.semaphore_wait(barrier, n_ga - 1 + n_col)

    @pl.loop(1, n_ga)
    def _(d):
        to = lax.rem(me_g + n_ga // 2 + d, n_ga)
        to = jnp.where(to == me_g, lax.rem(me_g + n_ga // 2, n_ga), to)
        send(cols_send, cols_recv.at[me_g], 0, cols_sem.at[me_t], ga=to)
        send(z_send.at[to], z_recv.at[me_g], 1, z_sem.at[me_t], ga=to)

    @pl.loop(0, tiles)
    def _(step):
        t = tile_at(step)
        base = per_tile * t
        wait_bytes(cols_recv.at[pl.ds(base, per_tile)], cols_sem.at[t])
        col = jnp.concatenate(
            [cols_recv[base + i] + cols_recv[base + i + 1] for i in range(0, per_tile, 2)], axis=1
        )
        kx, ky = lax.shift_right_logical(col, 8), col & (GRID - 1)
        row = jnp.where(kx < GRID // 2, kx + RADIUS, kx + RADIUS - GRID)
        onehot_x[t] = (iota((ROWS, TILE), 0) == row).astype(F32).astype(BF16)
        onehot_y = (iota((GRID, TILE), 0) == ky).astype(F32).astype(BF16)
        table_y[t] = dot(table_v[...], onehot_y, 1, 0).astype(BF16)
        wait_bytes(z_recv.at[pl.ds(base, per_tile)], z_sem.at[t])
        z = jnp.concatenate([swap(*z_pair(base + i)) for i in range(0, per_tile, 2)], axis=1)
        pick = onehot_x[t].reshape(ROWS // 16, 16, TILE)
        spread = jnp.concatenate(
            [
                (pick * jnp.broadcast_to(z[p : p + 1], (16, TILE)).astype(BF16)[None]).reshape(
                    ROWS, TILE
                )
                for p in range(planes)
            ],
            axis=0,
        )
        half_acc[...] += dot(spread, table_y[t], 1, 1).reshape(planes, ROWS, GRID)

    take(5, 6, 7)

    @pl.loop(0, planes, unroll=UNROLL)
    def _(p):
        field = dot(disc_t_v[...], half_acc[p].astype(BF16), 1, 0)
        pot_v[p] = (pot_v[p].astype(F32) * field).astype(BF16)

    @pl.loop(0, planes, unroll=UNROLL)
    def _(p):
        back_v[p] = dot(disc_v[...], pot_v[p], 1, 0).astype(BF16)

    @pl.loop(0, tiles)
    def _(step):
        t = tile_at(tiles - 1 - step)
        spectrum = dot(back_v[...].reshape(planes * ROWS, GRID), table_y[t], 1, 0)
        picked = (spectrum.reshape(planes, ROWS, TILE) * onehot_x[t].astype(F32)[None]).sum(axis=1)
        picked = picked.astype(BF16).astype(F32)
        for i in range(per_tile // 2):
            pair = per_tile // 2 * t + i
            rows = picked[:, 2 * sticks * i : 2 * sticks * (i + 1)]
            low = iota((half, 2 * sticks), 1) < sticks
            lower, upper = rows[:half], rows[half:]
            pick_send[2 * pair] = jnp.where(low, lower, pltpu.roll(upper, sticks, 1))
            pick_send[2 * pair + 1] = jnp.where(low, pltpu.roll(lower, sticks, 1), upper)
        for i in range(per_tile):
            to = per_tile * t + (i + me_g) % per_tile

            @pl.when(to != me_g)
            def _():
                send(pick_send.at[to], pick_recv.at[me_g], 2, pick_sem.at[0], ga=to)

    pltpu.make_async_copy(pick_send.at[me_g], pick_recv.at[me_g], pick_sem.at[0]).start()

    def packed(low, high):
        lane = iota(low.shape, low.ndim - 1)
        spare = (lane == RADIUS) & (counts < 2 * RADIUS + 1)
        return jnp.where(
            lane < RADIUS, low, jnp.where(spare, pltpu.roll(low, 1, low.ndim - 2), high)
        )

    take(8)

    @pl.loop(0, n_res)
    def _(r):
        rows = res_v[r].astype(F32)
        packed_res[r] = packed(rows[:, : GRID // 2], rows[:, GRID // 2 :]).astype(BF16)

    wait_bytes(pick_recv, pick_sem.at[0])
    returned = pick_recv[...].reshape(n_planes // 2, 2 * sticks)
    returned = jnp.concatenate([returned[:, :sticks], returned[:, sticks:]], axis=0)
    result = dot(returned.astype(BF16), ztab_v[...], 0, 0)
    result = jnp.where(sphere, result, 0.0)
    gather[core, column] = packed(result[:, : GRID // 2], result[:, GRID // 2 :]).astype(BF16)

    for dz in range(min(2, n_col) - 1, -1, -1):
        for dx in [i for i in (2, 1, 3, 0) if i < n_col // 2 or i == 0]:
            if dx == 0 and dz == 0:
                continue
            q = column_of(column, n_col, dx, dz)
            slot = gather.at[core, column]
            send(slot, slot, 3, gather_sem.at[0, 2 * dx + dz], band=2 * q + core)
    slot = gather.at[core, column]
    send(slot, slot, 3, gather_sem.at[1, 0], band=other)
    out_v[...] = result.astype(BF16)
    store = pltpu.make_async_copy(out_v, applied_ref, out_sem.at[0])
    store.start()
    offsets = [
        (dx, dz)
        for dx, dz in ((1, 0), (3, 0), (0, 1), (2, 0), (1, 1), (3, 1), (2, 1))
        if (dx < n_col // 2 or dx == 0) and dz < n_col
    ]
    for dx, dz in offsets:
        q = column_of(column, n_col, -dx, dz)
        slot = gather.at[core, q]
        wait_bytes(slot, gather_sem.at[0, 2 * dx + dz])
        send(slot, slot, 3, gather_sem.at[1, 2 * dx + dz], band=other)

    def products(which):
        prod = jnp.zeros((n_res * 16, n_col * 16), F32)
        for g in range(sticks // 16):
            left = packed_res[:, 16 * g : 16 * g + 16, :].reshape(n_res * 16, GRID // 2)
            right = gather[which, :, 16 * g : 16 * g + 16, :].reshape(n_col * 16, GRID // 2)
            prod += dot(left, right, 1, 1)
        same = iota(prod.shape, 0) % 16 == iota(prod.shape, 1) % 16
        summed = jnp.where(same, prod, 0.0).reshape(n_res, 16, n_col * 16).sum(axis=1)
        band = iota((n_col * 16, 128), 0) // 16 * 2 + which
        fold = (band == iota((n_col * 16, 128), 1) % 16).astype(F32)
        return dot(summed, fold, 1, 0, EXACT)

    part = products(core)
    for dx, dz in [(0, 0)] + offsets:
        q = column_of(column, n_col, -dx, dz)
        wait_bytes(gather.at[1 - core, q], gather_sem.at[1, 2 * dx + dz])
    part += products(1 - core)
    part = jnp.where(iota(part.shape, 1) // 16 == iota(part.shape, 0) % 8, part, 0.0)
    red_send[...] = part.reshape(n_res // 8, 8, 128).sum(axis=1)
    pltpu.make_async_copy(red_send, red_recv.at[me_g], red_sem.at[0]).start()

    @pl.loop(1, n_ga)
    def _(d):
        to = lax.rem(me_g + d, n_ga)
        send(red_send, red_recv.at[me_g], 4, red_sem.at[0], ga=to)

    wait_bytes(red_recv, red_sem.at[0])
    store.wait()
    wait_bytes(cols_recv.at[pl.ds(0, n_ga - 1)], send_sem.at[0])
    wait_bytes(z_recv.at[pl.ds(0, n_ga - 1)], send_sem.at[1])
    wait_bytes(pick_recv.at[pl.ds(0, n_ga - 1)], send_sem.at[2])
    for _ in range(2):
        wait_bytes(gather.at[0, pl.ds(0, n_col - 1)], send_sem.at[3])
    wait_bytes(gather.at[0, 0], send_sem.at[3])
    wait_bytes(red_recv.at[pl.ds(0, n_ga - 1)], send_sem.at[4])


def column_of(column, n_col, dx, dz):
    if n_col == 1:
        return column
    n_x = n_col // 2
    x = lax.rem(column // 2 + dx + n_x, n_x)
    z = lax.rem(column % 2 + dz, 2)
    return 2 * x + z


def finish(applied_ref, parts_ref, applied_out, inter_out):
    applied_out[0] = applied_ref[...]
    n_res = inter_out.shape[0]
    total = parts_ref[...].sum(axis=0)
    total = jnp.broadcast_to(total[:, None, :], (n_res // 8, 8, 128)).reshape(n_res, 128)
    total = jnp.where(iota(total.shape, 1) // 16 == iota(total.shape, 0) % 8, total, 0.0)
    fold = (iota((128, 16), 0) % 16 == iota((128, 16), 1)).astype(F32)
    inter_out[...] = dot(total, fold, 1, 0, EXACT)


def body(n_band, n_ga, psi_block, potential, resident, stick_cols, stick_counts, plane_order):
    sticks, planes, n_res = psi_block.shape[1], potential.shape[0], resident.shape[0]
    tiles = n_ga * sticks // TILE
    table, disc, disc_t = hartley_tables()
    hbm = pl.BlockSpec(memory_space=pltpu.HBM)
    vmem = pl.BlockSpec(memory_space=pltpu.VMEM)
    applied, inter = pl.pallas_call(
        functools.partial(kernel, n_band, n_ga),
        out_shape=(
            jax.ShapeDtypeStruct((sticks, GRID), BF16),
            jax.ShapeDtypeStruct((n_ga, n_res // 8, 128), F32),
        ),
        in_specs=[hbm] * 9,
        out_specs=(hbm, hbm),
        scratch_shapes=[
            pltpu.VMEM((1, sticks), jnp.int32),
            pltpu.VMEM((1, sticks), jnp.int32),
            pltpu.VMEM((1, n_ga * planes), jnp.int32),
            pltpu.VMEM((sticks, GRID), BF16),
            pltpu.VMEM(potential.shape, BF16),
            pltpu.VMEM(resident.shape, BF16),
            pltpu.VMEM(table.shape, BF16),
            pltpu.VMEM(disc.shape, BF16),
            pltpu.VMEM(disc_t.shape, BF16),
            pltpu.VMEM((sticks, GRID), BF16),
            pltpu.VMEM((n_ga * planes, GRID), BF16),
            pltpu.VMEM((1, 2 * sticks), jnp.int32),
            pltpu.VMEM((n_ga, 1, 2 * sticks), jnp.int32),
            pltpu.VMEM((n_ga, planes // 2, 2 * sticks), F32),
            pltpu.VMEM((n_ga, planes // 2, 2 * sticks), F32),
            pltpu.VMEM((n_ga, planes // 2, 2 * sticks), F32),
            pltpu.VMEM((n_ga, planes // 2, 2 * sticks), F32),
            pltpu.VMEM((tiles, ROWS, TILE), BF16),
            pltpu.VMEM((tiles, GRID, TILE), BF16),
            pltpu.VMEM((planes, ROWS, GRID), F32),
            pltpu.VMEM((planes, ROWS, GRID), BF16),
            pltpu.VMEM((n_res, sticks, GRID // 2), BF16),
            pltpu.VMEM((2, n_band // 2, sticks, GRID // 2), BF16),
            pltpu.VMEM((n_res // 8, 128), F32),
            pltpu.SemaphoreType.DMA((9,)),
            pltpu.SemaphoreType.DMA((5,)),
            pltpu.SemaphoreType.DMA((tiles,)),
            pltpu.SemaphoreType.DMA((tiles,)),
            pltpu.SemaphoreType.DMA((1,)),
            pltpu.SemaphoreType.DMA((2, 8)),
            pltpu.SemaphoreType.DMA((1,)),
            pltpu.SemaphoreType.DMA((1,)),
        ],
        compiler_params=pltpu.CompilerParams(
            collective_id=0, has_side_effects=True, vmem_limit_bytes=VMEM_BYTES
        ),
    )(
        psi_block[0],
        potential,
        resident,
        stick_cols[None],
        stick_counts[None],
        plane_order[None],
        table,
        disc,
        disc_t,
    )
    applied, inter = pl.pallas_call(
        finish,
        out_shape=(
            jax.ShapeDtypeStruct((1, sticks, GRID), BF16),
            jax.ShapeDtypeStruct((n_res, 16), F32),
        ),
        in_specs=[vmem] * 2,
        out_specs=(vmem, vmem),
    )(applied, inter)
    return applied, inter[:, :n_band]


def solution(mesh):
    in_specs = (
        P("band", "ga", None),
        P("ga", None, None),
        P("band", "ga", None),
        P("ga"),
        P("ga"),
        P(),
    )
    out_specs = (P("band", "ga", None), P("band", None))
    step = functools.partial(body, mesh.shape["band"], mesh.shape["ga"])
    return jax.shard_map(step, mesh=mesh, in_specs=in_specs, out_specs=out_specs, check_vma=False)
```

```python
import functools

import jax
import jax.numpy as jnp
import numpy as np
from jax import lax
from jax.experimental import pallas as pl
from jax.experimental.pallas import tpu as pltpu
from jax.sharding import PartitionSpec as P

MESH = pl.DeviceIdType.MESH
GRID = 256
RADIUS = 64
ROWS = 144
TILE = 256
F32 = jnp.float32
BF16 = jnp.bfloat16
EXACT = lax.Precision.HIGHEST
UNROLL = 8
VMEM_BYTES = 60 * 2**20


def hartley_tables():
    k = np.arange(GRID)
    angle = (k[:, None] * k[None, :] % GRID).astype(np.float32) * np.float32(2.0 * np.pi / GRID)
    table = ((np.cos(angle) + np.sin(angle)) * np.float32(1.0 / np.sqrt(GRID))).astype(BF16)
    disc = np.zeros((ROWS, GRID), BF16)
    disc[: 2 * RADIUS + 1] = table[np.arange(-RADIUS, RADIUS + 1) % GRID]
    return table, disc, np.ascontiguousarray(disc.T)


def iota(shape, axis):
    return lax.broadcasted_iota(jnp.int32, shape, axis)


def dot(a, b, ca, cb, precision=None):
    return lax.dot_general(
        a, b, (((ca,), (cb,)), ((), ())), precision=precision, preferred_element_type=F32
    )


def kernel(
    n_band,
    n_ga,
    psi_ref,
    pot_ref,
    res_ref,
    cols_ref,
    counts_ref,
    order_ref,
    table_ref,
    disc_ref,
    disc_t_ref,
    applied_ref,
    red_recv,
    cols_v,
    counts_v,
    order_v,
    psi_v,
    pot_v,
    res_v,
    table_v,
    disc_v,
    disc_t_v,
    out_v,
    ztab_v,
    cols_send,
    cols_recv,
    z_send,
    z_recv,
    pick_send,
    pick_recv,
    onehot_x,
    table_y,
    half_acc,
    back_v,
    packed_res,
    gather,
    red_send,
    load_sem,
    send_sem,
    cols_sem,
    z_sem,
    pick_sem,
    gather_sem,
    red_sem,
    out_sem,
):
    me_b, me_g = lax.axis_index("band"), lax.axis_index("ga")
    sticks, planes, n_res = psi_ref.shape[0], pot_ref.shape[0], res_ref.shape[0]
    per_tile = TILE // sticks
    tiles = n_ga // per_tile
    me_t = me_g // per_tile
    core, column = me_b % 2, me_b // 2
    n_col = n_band // 2
    parity = lax.rem(me_g, 2)

    barrier = pltpu.get_barrier_semaphore()

    @pl.loop(1, n_ga)
    def _(d):
        to = lax.rem(me_g + d, n_ga)
        pl.semaphore_signal(barrier, inc=1, device_id={"ga": to}, device_id_type=MESH)

    @pl.loop(1, n_col)
    def _(d):
        to = lax.rem(column + d, n_col) * 2 + core
        pl.semaphore_signal(barrier, inc=1, device_id={"band": to}, device_id_type=MESH)

    other = column * 2 + 1 - core
    pl.semaphore_signal(barrier, inc=1, device_id={"band": other}, device_id_type=MESH)

    loads = [
        pltpu.make_async_copy(src, dst, load_sem.at[i])
        for i, (src, dst) in enumerate(
            (
                (cols_ref, cols_v),
                (counts_ref, counts_v),
                (order_ref, order_v),
                (psi_ref, psi_v),
                (table_ref, table_v),
                (disc_ref, disc_v),
                (disc_t_ref, disc_t_v),
                (pot_ref, pot_v),
                (res_ref, res_v),
            )
        )
    ]
    for load in loads:
        load.start()
    taken = set()

    def take(*which):
        for i in which:
            loads[i].wait()
            taken.add(i)

    def send(src, dst, phase, sem, **to):
        pltpu.make_async_remote_copy(
            src_ref=src,
            dst_ref=dst,
            send_sem=send_sem.at[phase],
            recv_sem=sem,
            device_id=to,
            device_id_type=MESH,
        ).start()

    def wait_bytes(ref, sem):
        pltpu.make_async_copy(ref, ref, sem).wait()

    def swap(even, odd):
        low = iota(even.shape, 1) < sticks
        lower = jnp.where(low, even, pltpu.roll(odd, sticks, 1))
        upper = jnp.where(low, pltpu.roll(even, sticks, 1), odd)
        return jnp.concatenate([lower, upper], axis=0)

    def z_pair(i):
        return z_recv[i], z_recv[i + 1]

    def tile_at(step):
        ahead = jnp.where(step % 2 == 1, (step + 1) // 2, tiles - step // 2)
        return lax.rem(me_t + ahead, tiles)

    take(0, 1, 2)
    counts = jnp.where(
        iota((sticks, sticks), 0) == iota((sticks, sticks), 1), counts_v[...].astype(F32), 0.0
    ).sum(axis=1, keepdims=True)
    k = iota((sticks, GRID), 1)
    freq = jnp.where(k < GRID // 2, k, GRID - k)
    sphere = (2 * freq + 1).astype(F32) <= counts

    lane_half = iota((1, 2 * sticks), 1) // sticks
    own_half = lane_half == parity
    cols = cols_v[...]
    cols_send[...] = jnp.where(own_half, jnp.concatenate([cols, cols], axis=1), 0)
    pltpu.make_async_copy(cols_send, cols_recv.at[me_g], cols_sem.at[me_t]).start()

    take(3, 4)
    n_planes, half = n_ga * planes, planes // 2
    q = iota((n_planes, n_planes), 1)
    moved = q % (n_planes // 2) // half * planes + q // (n_planes // 2) * half + q % half
    move = (iota((n_planes, n_planes), 0) == moved).astype(F32).astype(BF16)
    order = jnp.broadcast_to(order_v[...].astype(F32).astype(BF16), (16, n_planes))
    order = dot(order, move, 1, 0)[:1].astype(jnp.int32)
    order_pick = (iota((GRID, n_planes), 0) == order).astype(F32).astype(BF16)
    ztab = dot(order_pick, table_v[...], 0, 0).astype(BF16)
    ztab_v[...] = ztab
    masked = jnp.where(sphere, psi_v[...].astype(F32), 0.0).astype(BF16)
    zreal = dot(ztab, masked, 1, 1).astype(BF16).astype(F32)
    zreal = jnp.concatenate([zreal[: n_planes // 2], zreal[n_planes // 2 :]], axis=1)
    z_send[...] = zreal.reshape(n_ga, half, 2 * sticks)
    pltpu.make_async_copy(z_send.at[me_g], z_recv.at[me_g], z_sem.at[me_t]).start()
    half_acc[...] = jnp.zeros_like(half_acc)

    pl.semaphore_wait(barrier, n_ga - 1 + n_col)

    @pl.loop(1, n_ga)
    def _(d):
        to = lax.rem(me_g + n_ga // 2 + d, n_ga)
        to = jnp.where(to == me_g, lax.rem(me_g + n_ga // 2, n_ga), to)
        send(cols_send, cols_recv.at[me_g], 0, cols_sem.at[me_t], ga=to)
        send(z_send.at[to], z_recv.at[me_g], 1, z_sem.at[me_t], ga=to)

    @pl.loop(0, tiles)
    def _(step):
        t = tile_at(step)
        base = per_tile * t
        wait_bytes(cols_recv.at[pl.ds(base, per_tile)], cols_sem.at[t])
        col = jnp.concatenate(
            [cols_recv[base + i] + cols_recv[base + i + 1] for i in range(0, per_tile, 2)], axis=1
        )
        kx, ky = lax.shift_right_logical(col, 8), col & (GRID - 1)
        row = jnp.where(kx < GRID // 2, kx + RADIUS, kx + RADIUS - GRID)
        onehot_x[t] = (iota((ROWS, TILE), 0) == row).astype(F32).astype(BF16)
        onehot_y = (iota((GRID, TILE), 0) == ky).astype(F32).astype(BF16)
        table_y[t] = dot(table_v[...], onehot_y, 1, 0).astype(BF16)
        wait_bytes(z_recv.at[pl.ds(base, per_tile)], z_sem.at[t])
        z = jnp.concatenate([swap(*z_pair(base + i)) for i in range(0, per_tile, 2)], axis=1)
        pick = onehot_x[t].reshape(ROWS // 16, 16, TILE)
        spread = jnp.concatenate(
            [
                (pick * jnp.broadcast_to(z[p : p + 1], (16, TILE)).astype(BF16)[None]).reshape(
                    ROWS, TILE
                )
                for p in range(planes)
            ],
            axis=0,
        )
        half_acc[...] += dot(spread, table_y[t], 1, 1).reshape(planes, ROWS, GRID)

    take(5, 6, 7)

    @pl.loop(0, planes, unroll=UNROLL)
    def _(p):
        field = dot(disc_t_v[...], half_acc[p].astype(BF16), 1, 0)
        pot_v[p] = (pot_v[p].astype(F32) * field).astype(BF16)

    @pl.loop(0, planes, unroll=UNROLL)
    def _(p):
        back_v[p] = dot(disc_v[...], pot_v[p], 1, 0).astype(BF16)

    @pl.loop(0, tiles)
    def _(step):
        t = tile_at(tiles - 1 - step)
        spectrum = dot(back_v[...].reshape(planes * ROWS, GRID), table_y[t], 1, 0)
        picked = (spectrum.reshape(planes, ROWS, TILE) * onehot_x[t].astype(F32)[None]).sum(axis=1)
        picked = picked.astype(BF16).astype(F32)
        for i in range(per_tile // 2):
            pair = per_tile // 2 * t + i
            rows = picked[:, 2 * sticks * i : 2 * sticks * (i + 1)]
            low = iota((half, 2 * sticks), 1) < sticks
            lower, upper = rows[:half], rows[half:]
            pick_send[2 * pair] = jnp.where(low, lower, pltpu.roll(upper, sticks, 1))
            pick_send[2 * pair + 1] = jnp.where(low, pltpu.roll(lower, sticks, 1), upper)
        for i in range(per_tile):
            to = per_tile * t + (i + me_g) % per_tile

            @pl.when(to != me_g)
            def _():
                send(pick_send.at[to], pick_recv.at[me_g], 2, pick_sem.at[0], ga=to)

    pltpu.make_async_copy(pick_send.at[me_g], pick_recv.at[me_g], pick_sem.at[0]).start()

    def packed(low, high):
        lane = iota(low.shape, low.ndim - 1)
        spare = (lane == RADIUS) & (counts < 2 * RADIUS + 1)
        return jnp.where(
            lane < RADIUS, low, jnp.where(spare, pltpu.roll(low, 1, low.ndim - 2), high)
        )

    take(8)

    @pl.loop(0, n_res)
    def _(r):
        rows = res_v[r].astype(F32)
        packed_res[r] = packed(rows[:, : GRID // 2], rows[:, GRID // 2 :]).astype(BF16)

    wait_bytes(pick_recv, pick_sem.at[0])
    returned = pick_recv[...].reshape(n_planes // 2, 2 * sticks)
    returned = jnp.concatenate([returned[:, :sticks], returned[:, sticks:]], axis=0)
    result = dot(returned.astype(BF16), ztab_v[...], 0, 0)
    result = jnp.where(sphere, result, 0.0)
    gather[core, column] = packed(result[:, : GRID // 2], result[:, GRID // 2 :]).astype(BF16)

    for dz in range(min(2, n_col) - 1, -1, -1):
        for dx in [i for i in (2, 1, 3, 0) if i < n_col // 2 or i == 0]:
            if dx == 0 and dz == 0:
                continue
            q = column_of(column, n_col, dx, dz)
            slot = gather.at[core, column]
            send(slot, slot, 3, gather_sem.at[0, 2 * dx + dz], band=2 * q + core)
    slot = gather.at[core, column]
    send(slot, slot, 3, gather_sem.at[1, 0], band=other)
    out_v[...] = result.astype(BF16)
    store = pltpu.make_async_copy(out_v, applied_ref, out_sem.at[0])
    store.start()
    offsets = [
        (dx, dz)
        for dx, dz in ((1, 0), (3, 0), (2, 0), (0, 1), (1, 1), (3, 1), (2, 1))
        if (dx < n_col // 2 or dx == 0) and dz < n_col
    ]
    for dx, dz in offsets:
        q = column_of(column, n_col, -dx, dz)
        slot = gather.at[core, q]
        wait_bytes(slot, gather_sem.at[0, 2 * dx + dz])
        send(slot, slot, 3, gather_sem.at[1, 2 * dx + dz], band=other)

    def products(which):
        prod = jnp.zeros((n_res * 16, n_col * 16), F32)
        for g in range(sticks // 16):
            left = packed_res[:, 16 * g : 16 * g + 16, :].reshape(n_res * 16, GRID // 2)
            right = gather[which, :, 16 * g : 16 * g + 16, :].reshape(n_col * 16, GRID // 2)
            prod += dot(left, right, 1, 1)
        same = iota(prod.shape, 0) % 16 == iota(prod.shape, 1) % 16
        summed = jnp.where(same, prod, 0.0).reshape(n_res, 16, n_col * 16).sum(axis=1)
        band = iota((n_col * 16, 128), 0) // 16 * 2 + which
        fold = (band == iota((n_col * 16, 128), 1) % 16).astype(F32)
        return dot(summed, fold, 1, 0, EXACT)

    part = products(core)
    for dx, dz in [(0, 0)] + offsets:
        q = column_of(column, n_col, -dx, dz)
        wait_bytes(gather.at[1 - core, q], gather_sem.at[1, 2 * dx + dz])
    part += products(1 - core)
    part = jnp.where(iota(part.shape, 1) // 16 == iota(part.shape, 0) % 8, part, 0.0)
    red_send[...] = part.reshape(n_res // 8, 8, 128).sum(axis=1)
    pltpu.make_async_copy(red_send, red_recv.at[me_g], red_sem.at[0]).start()

    @pl.loop(1, n_ga)
    def _(d):
        to = lax.rem(me_g + d, n_ga)
        send(red_send, red_recv.at[me_g], 4, red_sem.at[0], ga=to)

    wait_bytes(red_recv, red_sem.at[0])
    store.wait()
    wait_bytes(cols_recv.at[pl.ds(0, n_ga - 1)], send_sem.at[0])
    wait_bytes(z_recv.at[pl.ds(0, n_ga - 1)], send_sem.at[1])
    wait_bytes(pick_recv.at[pl.ds(0, n_ga - 1)], send_sem.at[2])
    for _ in range(2):
        wait_bytes(gather.at[0, pl.ds(0, n_col - 1)], send_sem.at[3])
    wait_bytes(gather.at[0, 0], send_sem.at[3])
    wait_bytes(red_recv.at[pl.ds(0, n_ga - 1)], send_sem.at[4])


def column_of(column, n_col, dx, dz):
    if n_col == 1:
        return column
    n_x = n_col // 2
    x = lax.rem(column // 2 + dx + n_x, n_x)
    z = lax.rem(column % 2 + dz, 2)
    return 2 * x + z


def finish(applied_ref, parts_ref, applied_out, inter_out):
    applied_out[0] = applied_ref[...]
    n_res = inter_out.shape[0]
    total = parts_ref[...].sum(axis=0)
    total = jnp.broadcast_to(total[:, None, :], (n_res // 8, 8, 128)).reshape(n_res, 128)
    total = jnp.where(iota(total.shape, 1) // 16 == iota(total.shape, 0) % 8, total, 0.0)
    fold = (iota((128, 16), 0) % 16 == iota((128, 16), 1)).astype(F32)
    inter_out[...] = dot(total, fold, 1, 0, EXACT)


def body(n_band, n_ga, psi_block, potential, resident, stick_cols, stick_counts, plane_order):
    sticks, planes, n_res = psi_block.shape[1], potential.shape[0], resident.shape[0]
    tiles = n_ga * sticks // TILE
    table, disc, disc_t = hartley_tables()
    hbm = pl.BlockSpec(memory_space=pltpu.HBM)
    vmem = pl.BlockSpec(memory_space=pltpu.VMEM)
    applied, inter = pl.pallas_call(
        functools.partial(kernel, n_band, n_ga),
        out_shape=(
            jax.ShapeDtypeStruct((sticks, GRID), BF16),
            jax.ShapeDtypeStruct((n_ga, n_res // 8, 128), F32),
        ),
        in_specs=[hbm] * 9,
        out_specs=(hbm, hbm),
        scratch_shapes=[
            pltpu.VMEM((1, sticks), jnp.int32),
            pltpu.VMEM((1, sticks), jnp.int32),
            pltpu.VMEM((1, n_ga * planes), jnp.int32),
            pltpu.VMEM((sticks, GRID), BF16),
            pltpu.VMEM(potential.shape, BF16),
            pltpu.VMEM(resident.shape, BF16),
            pltpu.VMEM(table.shape, BF16),
            pltpu.VMEM(disc.shape, BF16),
            pltpu.VMEM(disc_t.shape, BF16),
            pltpu.VMEM((sticks, GRID), BF16),
            pltpu.VMEM((n_ga * planes, GRID), BF16),
            pltpu.VMEM((1, 2 * sticks), jnp.int32),
            pltpu.VMEM((n_ga, 1, 2 * sticks), jnp.int32),
            pltpu.VMEM((n_ga, planes // 2, 2 * sticks), F32),
            pltpu.VMEM((n_ga, planes // 2, 2 * sticks), F32),
            pltpu.VMEM((n_ga, planes // 2, 2 * sticks), F32),
            pltpu.VMEM((n_ga, planes // 2, 2 * sticks), F32),
            pltpu.VMEM((tiles, ROWS, TILE), BF16),
            pltpu.VMEM((tiles, GRID, TILE), BF16),
            pltpu.VMEM((planes, ROWS, GRID), F32),
            pltpu.VMEM((planes, ROWS, GRID), BF16),
            pltpu.VMEM((n_res, sticks, GRID // 2), BF16),
            pltpu.VMEM((2, n_band // 2, sticks, GRID // 2), BF16),
            pltpu.VMEM((n_res // 8, 128), F32),
            pltpu.SemaphoreType.DMA((9,)),
            pltpu.SemaphoreType.DMA((5,)),
            pltpu.SemaphoreType.DMA((tiles,)),
            pltpu.SemaphoreType.DMA((tiles,)),
            pltpu.SemaphoreType.DMA((1,)),
            pltpu.SemaphoreType.DMA((2, 8)),
            pltpu.SemaphoreType.DMA((1,)),
            pltpu.SemaphoreType.DMA((1,)),
        ],
        compiler_params=pltpu.CompilerParams(
            collective_id=0, has_side_effects=True, vmem_limit_bytes=VMEM_BYTES
        ),
    )(
        psi_block[0],
        potential,
        resident,
        stick_cols[None],
        stick_counts[None],
        plane_order[None],
        table,
        disc,
        disc_t,
    )
    applied, inter = pl.pallas_call(
        finish,
        out_shape=(
            jax.ShapeDtypeStruct((1, sticks, GRID), BF16),
            jax.ShapeDtypeStruct((n_res, 16), F32),
        ),
        in_specs=[vmem] * 2,
        out_specs=(vmem, vmem),
    )(applied, inter)
    return applied, inter[:, :n_band]


def solution(mesh):
    in_specs = (
        P("band", "ga", None),
        P("ga", None, None),
        P("band", "ga", None),
        P("ga"),
        P("ga"),
        P(),
    )
    out_specs = (P("band", "ga", None), P("band", None))
    step = functools.partial(body, mesh.shape["band"], mesh.shape["ga"])
    return jax.shard_map(step, mesh=mesh, in_specs=in_specs, out_specs=out_specs, check_vma=False)
```

```python
import functools

import jax
import jax.numpy as jnp
import numpy as np
from jax import lax
from jax.experimental import pallas as pl
from jax.experimental.pallas import tpu as pltpu
from jax.sharding import PartitionSpec as P

MESH = pl.DeviceIdType.MESH
GRID = 256
RADIUS = 64
ROWS = 144
TILE = 256
F32 = jnp.float32
BF16 = jnp.bfloat16
EXACT = lax.Precision.HIGHEST
UNROLL = 8
VMEM_BYTES = 60 * 2**20


def hartley_tables():
    k = np.arange(GRID)
    angle = (k[:, None] * k[None, :] % GRID).astype(np.float32) * np.float32(2.0 * np.pi / GRID)
    table = ((np.cos(angle) + np.sin(angle)) * np.float32(1.0 / np.sqrt(GRID))).astype(BF16)
    disc = np.zeros((ROWS, GRID), BF16)
    disc[: 2 * RADIUS + 1] = table[np.arange(-RADIUS, RADIUS + 1) % GRID]
    return table, disc, np.ascontiguousarray(disc.T)


def iota(shape, axis):
    return lax.broadcasted_iota(jnp.int32, shape, axis)


def dot(a, b, ca, cb, precision=None):
    return lax.dot_general(
        a, b, (((ca,), (cb,)), ((), ())), precision=precision, preferred_element_type=F32
    )


def kernel(
    n_band,
    n_ga,
    psi_ref,
    pot_ref,
    res_ref,
    cols_ref,
    counts_ref,
    order_ref,
    table_ref,
    disc_ref,
    disc_t_ref,
    applied_ref,
    red_recv,
    cols_v,
    counts_v,
    order_v,
    psi_v,
    pot_v,
    res_v,
    table_v,
    disc_v,
    disc_t_v,
    out_v,
    ztab_v,
    cols_send,
    cols_recv,
    z_send,
    z_recv,
    pick_send,
    pick_recv,
    onehot_x,
    table_y,
    half_acc,
    back_v,
    packed_res,
    gather,
    red_send,
    load_sem,
    send_sem,
    cols_sem,
    z_sem,
    pick_sem,
    gather_sem,
    red_sem,
    out_sem,
):
    me_b, me_g = lax.axis_index("band"), lax.axis_index("ga")
    sticks, planes, n_res = psi_ref.shape[0], pot_ref.shape[0], res_ref.shape[0]
    per_tile = TILE // sticks
    tiles = n_ga // per_tile
    me_t = me_g // per_tile
    core, column = me_b % 2, me_b // 2
    n_col = n_band // 2
    parity = lax.rem(me_g, 2)

    far = (2, 1) if n_col == 8 else None
    barrier = pltpu.get_barrier_semaphore()

    @pl.loop(1, n_ga)
    def _(d):
        to = lax.rem(me_g + d, n_ga)
        pl.semaphore_signal(barrier, inc=1, device_id={"ga": to}, device_id_type=MESH)

    @pl.loop(1, n_col)
    def _(d):
        to = lax.rem(column + d, n_col) * 2 + core
        pl.semaphore_signal(barrier, inc=1, device_id={"band": to}, device_id_type=MESH)

    if far is not None:
        to = 2 * column_of(column, n_col, *far) + 1 - core
        pl.semaphore_signal(barrier, inc=1, device_id={"band": to}, device_id_type=MESH)
    other = column * 2 + 1 - core
    pl.semaphore_signal(barrier, inc=1, device_id={"band": other}, device_id_type=MESH)

    loads = [
        pltpu.make_async_copy(src, dst, load_sem.at[i])
        for i, (src, dst) in enumerate(
            (
                (cols_ref, cols_v),
                (counts_ref, counts_v),
                (order_ref, order_v),
                (psi_ref, psi_v),
                (table_ref, table_v),
                (disc_ref, disc_v),
                (disc_t_ref, disc_t_v),
                (pot_ref, pot_v),
                (res_ref, res_v),
            )
        )
    ]
    for load in loads:
        load.start()
    taken = set()

    def take(*which):
        for i in which:
            loads[i].wait()
            taken.add(i)

    def send(src, dst, phase, sem, **to):
        pltpu.make_async_remote_copy(
            src_ref=src,
            dst_ref=dst,
            send_sem=send_sem.at[phase],
            recv_sem=sem,
            device_id=to,
            device_id_type=MESH,
        ).start()

    def wait_bytes(ref, sem):
        pltpu.make_async_copy(ref, ref, sem).wait()

    def swap(even, odd):
        low = iota(even.shape, 1) < sticks
        lower = jnp.where(low, even, pltpu.roll(odd, sticks, 1))
        upper = jnp.where(low, pltpu.roll(even, sticks, 1), odd)
        return jnp.concatenate([lower, upper], axis=0)

    def z_pair(i):
        return z_recv[i], z_recv[i + 1]

    def tile_at(step):
        ahead = jnp.where(step % 2 == 1, (step + 1) // 2, tiles - step // 2)
        return lax.rem(me_t + ahead, tiles)

    take(0, 1, 2)
    counts = jnp.where(
        iota((sticks, sticks), 0) == iota((sticks, sticks), 1), counts_v[...].astype(F32), 0.0
    ).sum(axis=1, keepdims=True)
    k = iota((sticks, GRID), 1)
    freq = jnp.where(k < GRID // 2, k, GRID - k)
    sphere = (2 * freq + 1).astype(F32) <= counts

    lane_half = iota((1, 2 * sticks), 1) // sticks
    own_half = lane_half == parity
    cols = cols_v[...]
    cols_send[...] = jnp.where(own_half, jnp.concatenate([cols, cols], axis=1), 0)
    pltpu.make_async_copy(cols_send, cols_recv.at[me_g], cols_sem.at[me_t]).start()

    take(3, 4)
    n_planes, half = n_ga * planes, planes // 2
    q = iota((n_planes, n_planes), 1)
    moved = q % (n_planes // 2) // half * planes + q // (n_planes // 2) * half + q % half
    move = (iota((n_planes, n_planes), 0) == moved).astype(F32).astype(BF16)
    order = jnp.broadcast_to(order_v[...].astype(F32).astype(BF16), (16, n_planes))
    order = dot(order, move, 1, 0)[:1].astype(jnp.int32)
    order_pick = (iota((GRID, n_planes), 0) == order).astype(F32).astype(BF16)
    ztab = dot(order_pick, table_v[...], 0, 0).astype(BF16)
    ztab_v[...] = ztab
    masked = jnp.where(sphere, psi_v[...].astype(F32), 0.0).astype(BF16)
    zreal = dot(ztab, masked, 1, 1).astype(BF16).astype(F32)
    zreal = jnp.concatenate([zreal[: n_planes // 2], zreal[n_planes // 2 :]], axis=1)
    z_send[...] = zreal.reshape(n_ga, half, 2 * sticks)
    pltpu.make_async_copy(z_send.at[me_g], z_recv.at[me_g], z_sem.at[me_t]).start()
    half_acc[...] = jnp.zeros_like(half_acc)

    pl.semaphore_wait(barrier, n_ga - 1 + n_col + (far is not None))

    @pl.loop(1, n_ga)
    def _(d):
        to = lax.rem(me_g + n_ga // 2 + d, n_ga)
        to = jnp.where(to == me_g, lax.rem(me_g + n_ga // 2, n_ga), to)
        send(cols_send, cols_recv.at[me_g], 0, cols_sem.at[me_t], ga=to)
        send(z_send.at[to], z_recv.at[me_g], 1, z_sem.at[me_t], ga=to)

    @pl.loop(0, tiles)
    def _(step):
        t = tile_at(step)
        base = per_tile * t
        wait_bytes(cols_recv.at[pl.ds(base, per_tile)], cols_sem.at[t])
        col = jnp.concatenate(
            [cols_recv[base + i] + cols_recv[base + i + 1] for i in range(0, per_tile, 2)], axis=1
        )
        kx, ky = lax.shift_right_logical(col, 8), col & (GRID - 1)
        row = jnp.where(kx < GRID // 2, kx + RADIUS, kx + RADIUS - GRID)
        onehot_x[t] = (iota((ROWS, TILE), 0) == row).astype(F32).astype(BF16)
        onehot_y = (iota((GRID, TILE), 0) == ky).astype(F32).astype(BF16)
        table_y[t] = dot(table_v[...], onehot_y, 1, 0).astype(BF16)
        wait_bytes(z_recv.at[pl.ds(base, per_tile)], z_sem.at[t])
        z = jnp.concatenate([swap(*z_pair(base + i)) for i in range(0, per_tile, 2)], axis=1)
        pick = onehot_x[t].reshape(ROWS // 16, 16, TILE)
        spread = jnp.concatenate(
            [
                (pick * jnp.broadcast_to(z[p : p + 1], (16, TILE)).astype(BF16)[None]).reshape(
                    ROWS, TILE
                )
                for p in range(planes)
            ],
            axis=0,
        )
        half_acc[...] += dot(spread, table_y[t], 1, 1).reshape(planes, ROWS, GRID)

    take(5, 6, 7)

    @pl.loop(0, planes, unroll=UNROLL)
    def _(p):
        field = dot(disc_t_v[...], half_acc[p].astype(BF16), 1, 0)
        pot_v[p] = (pot_v[p].astype(F32) * field).astype(BF16)

    @pl.loop(0, planes, unroll=UNROLL)
    def _(p):
        back_v[p] = dot(disc_v[...], pot_v[p], 1, 0).astype(BF16)

    @pl.loop(0, tiles)
    def _(step):
        t = tile_at(tiles - 1 - step)
        spectrum = dot(back_v[...].reshape(planes * ROWS, GRID), table_y[t], 1, 0)
        picked = (spectrum.reshape(planes, ROWS, TILE) * onehot_x[t].astype(F32)[None]).sum(axis=1)
        picked = picked.astype(BF16).astype(F32)
        for i in range(per_tile // 2):
            pair = per_tile // 2 * t + i
            rows = picked[:, 2 * sticks * i : 2 * sticks * (i + 1)]
            low = iota((half, 2 * sticks), 1) < sticks
            lower, upper = rows[:half], rows[half:]
            pick_send[2 * pair] = jnp.where(low, lower, pltpu.roll(upper, sticks, 1))
            pick_send[2 * pair + 1] = jnp.where(low, pltpu.roll(lower, sticks, 1), upper)
        for i in range(per_tile):
            to = per_tile * t + (i + me_g) % per_tile

            @pl.when(to != me_g)
            def _():
                send(pick_send.at[to], pick_recv.at[me_g], 2, pick_sem.at[0], ga=to)

    pltpu.make_async_copy(pick_send.at[me_g], pick_recv.at[me_g], pick_sem.at[0]).start()

    def packed(low, high):
        lane = iota(low.shape, low.ndim - 1)
        spare = (lane == RADIUS) & (counts < 2 * RADIUS + 1)
        return jnp.where(
            lane < RADIUS, low, jnp.where(spare, pltpu.roll(low, 1, low.ndim - 2), high)
        )

    take(8)

    @pl.loop(0, n_res)
    def _(r):
        rows = res_v[r].astype(F32)
        packed_res[r] = packed(rows[:, : GRID // 2], rows[:, GRID // 2 :]).astype(BF16)

    wait_bytes(pick_recv, pick_sem.at[0])
    returned = pick_recv[...].reshape(n_planes // 2, 2 * sticks)
    returned = jnp.concatenate([returned[:, :sticks], returned[:, sticks:]], axis=0)
    result = dot(returned.astype(BF16), ztab_v[...], 0, 0)
    result = jnp.where(sphere, result, 0.0)
    gather[core, column] = packed(result[:, : GRID // 2], result[:, GRID // 2 :]).astype(BF16)

    for dz in range(min(2, n_col) - 1, -1, -1):
        for dx in [i for i in (2, 1, 3, 0) if i < n_col // 2 or i == 0]:
            if dx == 0 and dz == 0:
                continue
            q = column_of(column, n_col, dx, dz)
            slot = gather.at[core, column]
            send(slot, slot, 3, gather_sem.at[0, 2 * dx + dz], band=2 * q + core)
    slot = gather.at[core, column]
    if far is not None:
        q = column_of(column, n_col, *far)
        send(slot, slot, 3, gather_sem.at[1, 2 * far[0] + far[1]], band=2 * q + 1 - core)
    send(slot, slot, 3, gather_sem.at[1, 0], band=other)
    out_v[...] = result.astype(BF16)
    store = pltpu.make_async_copy(out_v, applied_ref, out_sem.at[0])
    store.start()
    offsets = [
        (dx, dz)
        for dx, dz in ((1, 0), (3, 0), (2, 0), (0, 1), (1, 1), (3, 1), (2, 1))
        if (dx < n_col // 2 or dx == 0) and dz < n_col
    ]
    for dx, dz in offsets:
        q = column_of(column, n_col, -dx, dz)
        slot = gather.at[core, q]
        wait_bytes(slot, gather_sem.at[0, 2 * dx + dz])
        if (dx, dz) != far:
            send(slot, slot, 3, gather_sem.at[1, 2 * dx + dz], band=other)

    def products(which):
        prod = jnp.zeros((n_res * 16, n_col * 16), F32)
        for g in range(sticks // 16):
            left = packed_res[:, 16 * g : 16 * g + 16, :].reshape(n_res * 16, GRID // 2)
            right = gather[which, :, 16 * g : 16 * g + 16, :].reshape(n_col * 16, GRID // 2)
            prod += dot(left, right, 1, 1)
        same = iota(prod.shape, 0) % 16 == iota(prod.shape, 1) % 16
        summed = jnp.where(same, prod, 0.0).reshape(n_res, 16, n_col * 16).sum(axis=1)
        band = iota((n_col * 16, 128), 0) // 16 * 2 + which
        fold = (band == iota((n_col * 16, 128), 1) % 16).astype(F32)
        return dot(summed, fold, 1, 0, EXACT)

    part = products(core)
    for dx, dz in [(0, 0)] + offsets:
        q = column_of(column, n_col, -dx, dz)
        wait_bytes(gather.at[1 - core, q], gather_sem.at[1, 2 * dx + dz])
    part += products(1 - core)
    part = jnp.where(iota(part.shape, 1) // 16 == iota(part.shape, 0) % 8, part, 0.0)
    red_send[...] = part.reshape(n_res // 8, 8, 128).sum(axis=1)
    pltpu.make_async_copy(red_send, red_recv.at[me_g], red_sem.at[0]).start()

    @pl.loop(1, n_ga)
    def _(d):
        to = lax.rem(me_g + d, n_ga)
        send(red_send, red_recv.at[me_g], 4, red_sem.at[0], ga=to)

    wait_bytes(red_recv, red_sem.at[0])
    store.wait()
    wait_bytes(cols_recv.at[pl.ds(0, n_ga - 1)], send_sem.at[0])
    wait_bytes(z_recv.at[pl.ds(0, n_ga - 1)], send_sem.at[1])
    wait_bytes(pick_recv.at[pl.ds(0, n_ga - 1)], send_sem.at[2])
    for _ in range(2):
        wait_bytes(gather.at[0, pl.ds(0, n_col - 1)], send_sem.at[3])
    wait_bytes(gather.at[0, 0], send_sem.at[3])
    wait_bytes(red_recv.at[pl.ds(0, n_ga - 1)], send_sem.at[4])


def column_of(column, n_col, dx, dz):
    if n_col == 1:
        return column
    n_x = n_col // 2
    x = lax.rem(column // 2 + dx + n_x, n_x)
    z = lax.rem(column % 2 + dz, 2)
    return 2 * x + z


def finish(applied_ref, parts_ref, applied_out, inter_out):
    applied_out[0] = applied_ref[...]
    n_res = inter_out.shape[0]
    total = parts_ref[...].sum(axis=0)
    total = jnp.broadcast_to(total[:, None, :], (n_res // 8, 8, 128)).reshape(n_res, 128)
    total = jnp.where(iota(total.shape, 1) // 16 == iota(total.shape, 0) % 8, total, 0.0)
    fold = (iota((128, 16), 0) % 16 == iota((128, 16), 1)).astype(F32)
    inter_out[...] = dot(total, fold, 1, 0, EXACT)


def body(n_band, n_ga, psi_block, potential, resident, stick_cols, stick_counts, plane_order):
    sticks, planes, n_res = psi_block.shape[1], potential.shape[0], resident.shape[0]
    tiles = n_ga * sticks // TILE
    table, disc, disc_t = hartley_tables()
    hbm = pl.BlockSpec(memory_space=pltpu.HBM)
    vmem = pl.BlockSpec(memory_space=pltpu.VMEM)
    applied, inter = pl.pallas_call(
        functools.partial(kernel, n_band, n_ga),
        out_shape=(
            jax.ShapeDtypeStruct((sticks, GRID), BF16),
            jax.ShapeDtypeStruct((n_ga, n_res // 8, 128), F32),
        ),
        in_specs=[hbm] * 9,
        out_specs=(hbm, hbm),
        scratch_shapes=[
            pltpu.VMEM((1, sticks), jnp.int32),
            pltpu.VMEM((1, sticks), jnp.int32),
            pltpu.VMEM((1, n_ga * planes), jnp.int32),
            pltpu.VMEM((sticks, GRID), BF16),
            pltpu.VMEM(potential.shape, BF16),
            pltpu.VMEM(resident.shape, BF16),
            pltpu.VMEM(table.shape, BF16),
            pltpu.VMEM(disc.shape, BF16),
            pltpu.VMEM(disc_t.shape, BF16),
            pltpu.VMEM((sticks, GRID), BF16),
            pltpu.VMEM((n_ga * planes, GRID), BF16),
            pltpu.VMEM((1, 2 * sticks), jnp.int32),
            pltpu.VMEM((n_ga, 1, 2 * sticks), jnp.int32),
            pltpu.VMEM((n_ga, planes // 2, 2 * sticks), F32),
            pltpu.VMEM((n_ga, planes // 2, 2 * sticks), F32),
            pltpu.VMEM((n_ga, planes // 2, 2 * sticks), F32),
            pltpu.VMEM((n_ga, planes // 2, 2 * sticks), F32),
            pltpu.VMEM((tiles, ROWS, TILE), BF16),
            pltpu.VMEM((tiles, GRID, TILE), BF16),
            pltpu.VMEM((planes, ROWS, GRID), F32),
            pltpu.VMEM((planes, ROWS, GRID), BF16),
            pltpu.VMEM((n_res, sticks, GRID // 2), BF16),
            pltpu.VMEM((2, n_band // 2, sticks, GRID // 2), BF16),
            pltpu.VMEM((n_res // 8, 128), F32),
            pltpu.SemaphoreType.DMA((9,)),
            pltpu.SemaphoreType.DMA((5,)),
            pltpu.SemaphoreType.DMA((tiles,)),
            pltpu.SemaphoreType.DMA((tiles,)),
            pltpu.SemaphoreType.DMA((1,)),
            pltpu.SemaphoreType.DMA((2, 8)),
            pltpu.SemaphoreType.DMA((1,)),
            pltpu.SemaphoreType.DMA((1,)),
        ],
        compiler_params=pltpu.CompilerParams(
            collective_id=0, has_side_effects=True, vmem_limit_bytes=VMEM_BYTES
        ),
    )(
        psi_block[0],
        potential,
        resident,
        stick_cols[None],
        stick_counts[None],
        plane_order[None],
        table,
        disc,
        disc_t,
    )
    applied, inter = pl.pallas_call(
        finish,
        out_shape=(
            jax.ShapeDtypeStruct((1, sticks, GRID), BF16),
            jax.ShapeDtypeStruct((n_res, 16), F32),
        ),
        in_specs=[vmem] * 2,
        out_specs=(vmem, vmem),
    )(applied, inter)
    return applied, inter[:, :n_band]


def solution(mesh):
    in_specs = (
        P("band", "ga", None),
        P("ga", None, None),
        P("band", "ga", None),
        P("ga"),
        P("ga"),
        P(),
    )
    out_specs = (P("band", "ga", None), P("band", None))
    step = functools.partial(body, mesh.shape["band"], mesh.shape["ga"])
    return jax.shard_map(step, mesh=mesh, in_specs=in_specs, out_specs=out_specs, check_vma=False)
```

```python
import functools

import jax
import jax.numpy as jnp
import numpy as np
from jax import lax
from jax.experimental import pallas as pl
from jax.experimental.pallas import tpu as pltpu
from jax.sharding import PartitionSpec as P

MESH = pl.DeviceIdType.MESH
GRID = 256
RADIUS = 64
ROWS = 144
TILE = 256
F32 = jnp.float32
BF16 = jnp.bfloat16
EXACT = lax.Precision.HIGHEST
UNROLL = 8
VMEM_BYTES = 60 * 2**20


def hartley_tables():
    k = np.arange(GRID)
    angle = (k[:, None] * k[None, :] % GRID).astype(np.float32) * np.float32(2.0 * np.pi / GRID)
    table = ((np.cos(angle) + np.sin(angle)) * np.float32(1.0 / np.sqrt(GRID))).astype(BF16)
    disc = np.zeros((ROWS, GRID), BF16)
    disc[: 2 * RADIUS + 1] = table[np.arange(-RADIUS, RADIUS + 1) % GRID]
    return table, disc, np.ascontiguousarray(disc.T)


def iota(shape, axis):
    return lax.broadcasted_iota(jnp.int32, shape, axis)


def dot(a, b, ca, cb, precision=None):
    return lax.dot_general(
        a, b, (((ca,), (cb,)), ((), ())), precision=precision, preferred_element_type=F32
    )


def kernel(
    n_band,
    n_ga,
    psi_ref,
    pot_ref,
    res_ref,
    cols_ref,
    counts_ref,
    order_ref,
    table_ref,
    disc_ref,
    disc_t_ref,
    applied_ref,
    red_recv,
    cols_v,
    counts_v,
    order_v,
    psi_v,
    pot_v,
    res_v,
    table_v,
    disc_v,
    disc_t_v,
    out_v,
    ztab_v,
    cols_send,
    cols_recv,
    z_send,
    z_recv,
    pick_send,
    pick_recv,
    onehot_x,
    table_y,
    half_acc,
    back_v,
    packed_res,
    gather,
    red_send,
    load_sem,
    send_sem,
    cols_sem,
    z_sem,
    pick_sem,
    gather_sem,
    red_sem,
    out_sem,
):
    me_b, me_g = lax.axis_index("band"), lax.axis_index("ga")
    sticks, planes, n_res = psi_ref.shape[0], pot_ref.shape[0], res_ref.shape[0]
    per_tile = TILE // sticks
    tiles = n_ga // per_tile
    me_t = me_g // per_tile
    core, column = me_b % 2, me_b // 2
    n_col = n_band // 2
    parity = lax.rem(me_g, 2)

    barrier = pltpu.get_barrier_semaphore()

    @pl.loop(1, n_ga)
    def _(d):
        to = lax.rem(me_g + d, n_ga)
        pl.semaphore_signal(barrier, inc=1, device_id={"ga": to}, device_id_type=MESH)

    @pl.loop(1, n_col)
    def _(d):
        to = lax.rem(column + d, n_col) * 2 + core
        pl.semaphore_signal(barrier, inc=1, device_id={"band": to}, device_id_type=MESH)

    other = column * 2 + 1 - core
    pl.semaphore_signal(barrier, inc=1, device_id={"band": other}, device_id_type=MESH)

    loads = [
        pltpu.make_async_copy(src, dst, load_sem.at[i])
        for i, (src, dst) in enumerate(
            (
                (cols_ref, cols_v),
                (counts_ref, counts_v),
                (order_ref, order_v),
                (psi_ref, psi_v),
                (table_ref, table_v),
                (disc_ref, disc_v),
                (disc_t_ref, disc_t_v),
                (pot_ref, pot_v),
                (res_ref, res_v),
            )
        )
    ]
    for load in loads:
        load.start()
    taken = set()

    def take(*which):
        for i in which:
            loads[i].wait()
            taken.add(i)

    def send(src, dst, phase, sem, **to):
        pltpu.make_async_remote_copy(
            src_ref=src,
            dst_ref=dst,
            send_sem=send_sem.at[phase],
            recv_sem=sem,
            device_id=to,
            device_id_type=MESH,
        ).start()

    def wait_bytes(ref, sem):
        pltpu.make_async_copy(ref, ref, sem).wait()

    def swap(even, odd):
        low = iota(even.shape, 1) < sticks
        lower = jnp.where(low, even, pltpu.roll(odd, sticks, 1))
        upper = jnp.where(low, pltpu.roll(even, sticks, 1), odd)
        return jnp.concatenate([lower, upper], axis=0)

    def z_pair(i):
        return z_recv[i], z_recv[i + 1]

    def tile_at(step):
        ahead = jnp.where(step % 2 == 1, (step + 1) // 2, tiles - step // 2)
        return lax.rem(me_t + ahead, tiles)

    take(0, 1, 2)
    counts = jnp.where(
        iota((sticks, sticks), 0) == iota((sticks, sticks), 1), counts_v[...].astype(F32), 0.0
    ).sum(axis=1, keepdims=True)
    k = iota((sticks, GRID), 1)
    freq = jnp.where(k < GRID // 2, k, GRID - k)
    sphere = (2 * freq + 1).astype(F32) <= counts

    lane_half = iota((1, 2 * sticks), 1) // sticks
    own_half = lane_half == parity
    cols = cols_v[...]
    cols_send[...] = jnp.where(own_half, jnp.concatenate([cols, cols], axis=1), 0)
    pltpu.make_async_copy(cols_send, cols_recv.at[me_g], cols_sem.at[me_t]).start()

    take(3, 4)
    n_planes, half = n_ga * planes, planes // 2
    q = iota((n_planes, n_planes), 1)
    moved = q % (n_planes // 2) // half * planes + q // (n_planes // 2) * half + q % half
    move = (iota((n_planes, n_planes), 0) == moved).astype(F32).astype(BF16)
    order = jnp.broadcast_to(order_v[...].astype(F32).astype(BF16), (16, n_planes))
    order = dot(order, move, 1, 0)[:1].astype(jnp.int32)
    order_pick = (iota((GRID, n_planes), 0) == order).astype(F32).astype(BF16)
    ztab = dot(order_pick, table_v[...], 0, 0).astype(BF16)
    ztab_v[...] = ztab
    masked = jnp.where(sphere, psi_v[...].astype(F32), 0.0).astype(BF16)
    zreal = dot(ztab, masked, 1, 1).astype(BF16).astype(F32)
    zreal = jnp.concatenate([zreal[: n_planes // 2], zreal[n_planes // 2 :]], axis=1)
    z_send[...] = zreal.reshape(n_ga, half, 2 * sticks)
    pltpu.make_async_copy(z_send.at[me_g], z_recv.at[me_g], z_sem.at[me_t]).start()

    pl.semaphore_wait(barrier, n_ga - 1 + n_col)

    def send_sticks(ahead):
        to = lax.rem(me_g + ahead, n_ga)
        send(cols_send, cols_recv.at[me_g], 0, cols_sem.at[me_t], ga=to)
        send(z_send.at[to], z_recv.at[me_g], 1, z_sem.at[me_t], ga=to)

    quarter = n_ga // 4
    pl.loop(quarter, 3 * quarter + 1)(send_sticks)
    half_acc[...] = jnp.zeros_like(half_acc)
    pl.loop(3 * quarter + 1, n_ga)(send_sticks)
    pl.loop(1, quarter)(send_sticks)

    @pl.loop(0, tiles)
    def _(step):
        t = tile_at(step)
        base = per_tile * t
        wait_bytes(cols_recv.at[pl.ds(base, per_tile)], cols_sem.at[t])
        col = jnp.concatenate(
            [cols_recv[base + i] + cols_recv[base + i + 1] for i in range(0, per_tile, 2)], axis=1
        )
        kx, ky = lax.shift_right_logical(col, 8), col & (GRID - 1)
        row = jnp.where(kx < GRID // 2, kx + RADIUS, kx + RADIUS - GRID)
        onehot_x[t] = (iota((ROWS, TILE), 0) == row).astype(F32).astype(BF16)
        onehot_y = (iota((GRID, TILE), 0) == ky).astype(F32).astype(BF16)
        table_y[t] = dot(table_v[...], onehot_y, 1, 0).astype(BF16)
        wait_bytes(z_recv.at[pl.ds(base, per_tile)], z_sem.at[t])
        z = jnp.concatenate([swap(*z_pair(base + i)) for i in range(0, per_tile, 2)], axis=1)
        pick = onehot_x[t].reshape(ROWS // 16, 16, TILE)
        spread = jnp.concatenate(
            [
                (pick * jnp.broadcast_to(z[p : p + 1], (16, TILE)).astype(BF16)[None]).reshape(
                    ROWS, TILE
                )
                for p in range(planes)
            ],
            axis=0,
        )
        half_acc[...] += dot(spread, table_y[t], 1, 1).reshape(planes, ROWS, GRID)

    take(5, 6, 7)

    @pl.loop(0, planes, unroll=UNROLL)
    def _(p):
        field = dot(disc_t_v[...], half_acc[p].astype(BF16), 1, 0)
        pot_v[p] = (pot_v[p].astype(F32) * field).astype(BF16)

    @pl.loop(0, planes, unroll=UNROLL)
    def _(p):
        back_v[p] = dot(disc_v[...], pot_v[p], 1, 0).astype(BF16)

    @pl.loop(0, tiles)
    def _(step):
        t = tile_at(tiles - 1 - step)
        spectrum = dot(back_v[...].reshape(planes * ROWS, GRID), table_y[t], 1, 0)
        picked = (spectrum.reshape(planes, ROWS, TILE) * onehot_x[t].astype(F32)[None]).sum(axis=1)
        picked = picked.astype(BF16).astype(F32)
        for i in range(per_tile // 2):
            pair = per_tile // 2 * t + i
            rows = picked[:, 2 * sticks * i : 2 * sticks * (i + 1)]
            low = iota((half, 2 * sticks), 1) < sticks
            lower, upper = rows[:half], rows[half:]
            pick_send[2 * pair] = jnp.where(low, lower, pltpu.roll(upper, sticks, 1))
            pick_send[2 * pair + 1] = jnp.where(low, pltpu.roll(lower, sticks, 1), upper)
        for i in range(per_tile):
            to = per_tile * t + (i + me_g) % per_tile

            @pl.when(to != me_g)
            def _():
                send(pick_send.at[to], pick_recv.at[me_g], 2, pick_sem.at[0], ga=to)

    pltpu.make_async_copy(pick_send.at[me_g], pick_recv.at[me_g], pick_sem.at[0]).start()

    def packed(low, high):
        lane = iota(low.shape, low.ndim - 1)
        spare = (lane == RADIUS) & (counts < 2 * RADIUS + 1)
        return jnp.where(
            lane < RADIUS, low, jnp.where(spare, pltpu.roll(low, 1, low.ndim - 2), high)
        )

    take(8)

    @pl.loop(0, n_res)
    def _(r):
        rows = res_v[r].astype(F32)
        packed_res[r] = packed(rows[:, : GRID // 2], rows[:, GRID // 2 :]).astype(BF16)

    wait_bytes(pick_recv, pick_sem.at[0])
    returned = pick_recv[...].reshape(n_planes // 2, 2 * sticks)
    returned = jnp.concatenate([returned[:, :sticks], returned[:, sticks:]], axis=0)
    result = dot(returned.astype(BF16), ztab_v[...], 0, 0)
    result = jnp.where(sphere, result, 0.0)
    gather[core, column] = packed(result[:, : GRID // 2], result[:, GRID // 2 :]).astype(BF16)

    for dz in range(min(2, n_col) - 1, -1, -1):
        for dx in [i for i in (2, 1, 3, 0) if i < n_col // 2 or i == 0]:
            if dx == 0 and dz == 0:
                continue
            q = column_of(column, n_col, dx, dz)
            slot = gather.at[core, column]
            send(slot, slot, 3, gather_sem.at[0, 2 * dx + dz], band=2 * q + core)
    slot = gather.at[core, column]
    send(slot, slot, 3, gather_sem.at[1, 0], band=other)
    out_v[...] = result.astype(BF16)
    store = pltpu.make_async_copy(out_v, applied_ref, out_sem.at[0])
    store.start()
    offsets = [
        (dx, dz)
        for dx, dz in ((1, 0), (3, 0), (2, 0), (0, 1), (1, 1), (3, 1), (2, 1))
        if (dx < n_col // 2 or dx == 0) and dz < n_col
    ]
    for dx, dz in offsets:
        q = column_of(column, n_col, -dx, dz)
        slot = gather.at[core, q]
        wait_bytes(slot, gather_sem.at[0, 2 * dx + dz])
        send(slot, slot, 3, gather_sem.at[1, 2 * dx + dz], band=other)

    def products(which):
        prod = jnp.zeros((n_res * 16, n_col * 16), F32)
        for g in range(sticks // 16):
            left = packed_res[:, 16 * g : 16 * g + 16, :].reshape(n_res * 16, GRID // 2)
            right = gather[which, :, 16 * g : 16 * g + 16, :].reshape(n_col * 16, GRID // 2)
            prod += dot(left, right, 1, 1)
        same = iota(prod.shape, 0) % 16 == iota(prod.shape, 1) % 16
        summed = jnp.where(same, prod, 0.0).reshape(n_res, 16, n_col * 16).sum(axis=1)
        band = iota((n_col * 16, 128), 0) // 16 * 2 + which
        fold = (band == iota((n_col * 16, 128), 1) % 16).astype(F32)
        return dot(summed, fold, 1, 0, EXACT)

    part = products(core)
    for dx, dz in [(0, 0)] + offsets:
        q = column_of(column, n_col, -dx, dz)
        wait_bytes(gather.at[1 - core, q], gather_sem.at[1, 2 * dx + dz])
    part += products(1 - core)
    part = jnp.where(iota(part.shape, 1) // 16 == iota(part.shape, 0) % 8, part, 0.0)
    red_send[...] = part.reshape(n_res // 8, 8, 128).sum(axis=1)
    pltpu.make_async_copy(red_send, red_recv.at[me_g], red_sem.at[0]).start()

    @pl.loop(1, n_ga)
    def _(d):
        to = lax.rem(me_g + d, n_ga)
        send(red_send, red_recv.at[me_g], 4, red_sem.at[0], ga=to)

    wait_bytes(red_recv, red_sem.at[0])
    store.wait()
    wait_bytes(cols_recv.at[pl.ds(0, n_ga - 1)], send_sem.at[0])
    wait_bytes(z_recv.at[pl.ds(0, n_ga - 1)], send_sem.at[1])
    wait_bytes(pick_recv.at[pl.ds(0, n_ga - 1)], send_sem.at[2])
    for _ in range(2):
        wait_bytes(gather.at[0, pl.ds(0, n_col - 1)], send_sem.at[3])
    wait_bytes(gather.at[0, 0], send_sem.at[3])
    wait_bytes(red_recv.at[pl.ds(0, n_ga - 1)], send_sem.at[4])


def column_of(column, n_col, dx, dz):
    if n_col == 1:
        return column
    n_x = n_col // 2
    x = lax.rem(column // 2 + dx + n_x, n_x)
    z = lax.rem(column % 2 + dz, 2)
    return 2 * x + z


def finish(applied_ref, parts_ref, applied_out, inter_out):
    applied_out[0] = applied_ref[...]
    n_res = inter_out.shape[0]
    total = parts_ref[...].sum(axis=0)
    total = jnp.broadcast_to(total[:, None, :], (n_res // 8, 8, 128)).reshape(n_res, 128)
    total = jnp.where(iota(total.shape, 1) // 16 == iota(total.shape, 0) % 8, total, 0.0)
    fold = (iota((128, 16), 0) % 16 == iota((128, 16), 1)).astype(F32)
    inter_out[...] = dot(total, fold, 1, 0, EXACT)


def body(n_band, n_ga, psi_block, potential, resident, stick_cols, stick_counts, plane_order):
    sticks, planes, n_res = psi_block.shape[1], potential.shape[0], resident.shape[0]
    tiles = n_ga * sticks // TILE
    table, disc, disc_t = hartley_tables()
    hbm = pl.BlockSpec(memory_space=pltpu.HBM)
    vmem = pl.BlockSpec(memory_space=pltpu.VMEM)
    applied, inter = pl.pallas_call(
        functools.partial(kernel, n_band, n_ga),
        out_shape=(
            jax.ShapeDtypeStruct((sticks, GRID), BF16),
            jax.ShapeDtypeStruct((n_ga, n_res // 8, 128), F32),
        ),
        in_specs=[hbm] * 9,
        out_specs=(hbm, hbm),
        scratch_shapes=[
            pltpu.VMEM((1, sticks), jnp.int32),
            pltpu.VMEM((1, sticks), jnp.int32),
            pltpu.VMEM((1, n_ga * planes), jnp.int32),
            pltpu.VMEM((sticks, GRID), BF16),
            pltpu.VMEM(potential.shape, BF16),
            pltpu.VMEM(resident.shape, BF16),
            pltpu.VMEM(table.shape, BF16),
            pltpu.VMEM(disc.shape, BF16),
            pltpu.VMEM(disc_t.shape, BF16),
            pltpu.VMEM((sticks, GRID), BF16),
            pltpu.VMEM((n_ga * planes, GRID), BF16),
            pltpu.VMEM((1, 2 * sticks), jnp.int32),
            pltpu.VMEM((n_ga, 1, 2 * sticks), jnp.int32),
            pltpu.VMEM((n_ga, planes // 2, 2 * sticks), F32),
            pltpu.VMEM((n_ga, planes // 2, 2 * sticks), F32),
            pltpu.VMEM((n_ga, planes // 2, 2 * sticks), F32),
            pltpu.VMEM((n_ga, planes // 2, 2 * sticks), F32),
            pltpu.VMEM((tiles, ROWS, TILE), BF16),
            pltpu.VMEM((tiles, GRID, TILE), BF16),
            pltpu.VMEM((planes, ROWS, GRID), F32),
            pltpu.VMEM((planes, ROWS, GRID), BF16),
            pltpu.VMEM((n_res, sticks, GRID // 2), BF16),
            pltpu.VMEM((2, n_band // 2, sticks, GRID // 2), BF16),
            pltpu.VMEM((n_res // 8, 128), F32),
            pltpu.SemaphoreType.DMA((9,)),
            pltpu.SemaphoreType.DMA((5,)),
            pltpu.SemaphoreType.DMA((tiles,)),
            pltpu.SemaphoreType.DMA((tiles,)),
            pltpu.SemaphoreType.DMA((1,)),
            pltpu.SemaphoreType.DMA((2, 8)),
            pltpu.SemaphoreType.DMA((1,)),
            pltpu.SemaphoreType.DMA((1,)),
        ],
        compiler_params=pltpu.CompilerParams(
            collective_id=0, has_side_effects=True, vmem_limit_bytes=VMEM_BYTES
        ),
    )(
        psi_block[0],
        potential,
        resident,
        stick_cols[None],
        stick_counts[None],
        plane_order[None],
        table,
        disc,
        disc_t,
    )
    applied, inter = pl.pallas_call(
        finish,
        out_shape=(
            jax.ShapeDtypeStruct((1, sticks, GRID), BF16),
            jax.ShapeDtypeStruct((n_res, 16), F32),
        ),
        in_specs=[vmem] * 2,
        out_specs=(vmem, vmem),
    )(applied, inter)
    return applied, inter[:, :n_band]


def solution(mesh):
    in_specs = (
        P("band", "ga", None),
        P("ga", None, None),
        P("band", "ga", None),
        P("ga"),
        P("ga"),
        P(),
    )
    out_specs = (P("band", "ga", None), P("band", None))
    step = functools.partial(body, mesh.shape["band"], mesh.shape["ga"])
    return jax.shard_map(step, mesh=mesh, in_specs=in_specs, out_specs=out_specs, check_vma=False)
```
